512 devices in a mesh: node: 64 (over y_hi, z, core), local: 8 (over x, y_lo).
Axes of the slice: x: 4, y: 8 (y_hi: 4, y_lo: 2; y = y_hi * 2 + y_lo), z: 8, core: 2. Of those that a mesh axis runs over, the one named last changes fastest.
Arguments:
- tokens: bfloat16 [81920, 4096], P(('node', 'local')), may hold values from -24 to 24
- out_grad: bfloat16 [81920, 4096], P(('node', 'local')), may hold values from -24 to 24
- up_codes: bfloat16 [4096, 256], P('local'), may hold values from -127 to 127
- up_scales: float32 [4096, 2], P('local'), may hold values from 0.000109375 to 0.0004375
- down_codes: bfloat16 [4096, 256], P('local'), may hold values from -127 to 127
- down_scales: float32 [4096, 2], P('local'), may hold values from 0.000109375 to 0.0004375
Outputs:
- input_grad: bfloat16 [81920, 4096], P(('node', 'local'))
- grad_up: float32 [4096, 256], P(('local', 'node'))
- grad_down: float32 [4096, 256], P(('local', 'node'))
The draws below stay inside these ranges and needn't reach their ends.
All inputs are finite; a program needn't handle non-finite values.
Results may differ from the reference program's by a relative error of at most 0.0075.
Values sent between devices are 32-bit elements; how exact they have to be, the bound alone decides.
No kernel may reach another device: no remote copies, remote signals or barrier semaphores. Data moves between devices by JAX's collectives and lax.ppermute only.
A program may use at most 128 MiB of HBM per device.

```python
import math
import jax
import jax.numpy as jnp
from jax import lax

D = 4096
BUCKET = 256
QBLOCK = 128
TOK_DEV = 160
NBLOCK = 2
TOKENS = 81920
N_NODE = 64
N_LOCAL = 8


def with_spikes(values, key, source, target, parts, factor):
    owner, partner = [(jnp.arange(values.shape[dim]) // (values.shape[dim] // parts)).reshape([-1 if axis == dim else 1 for axis in range(values.ndim)]) for dim in (source, target)]
    chosen = jax.random.permutation(key, parts)[partner]
    strong = (owner == chosen) | (owner == (partner + parts // 2) % parts)
    return jnp.where(strong, factor * values, values)


def levels(stream_key, shape, pieces, low, largest):
    gain, own = 1.0, jax.random.fold_in(stream_key, 6)
    for axis_at, parts in pieces:
        steps = jnp.exp(jax.random.uniform(jax.random.fold_in(own, axis_at), (parts,), jnp.float32, low / len(pieces), largest / len(pieces)))
        gain = gain * jnp.repeat(steps, shape[axis_at] // parts).reshape([-1 if axis == axis_at else 1 for axis in range(len(shape))])
    return gain


def bell_draw_with(own_key, extent, spread, limit, pieces, heavy, kind=jnp.bfloat16):
    result = spread * jax.random.normal(own_key, extent, jnp.float32)
    if pieces:
        result = result * levels(own_key, extent, pieces, -0.22, 0.18)
    return jnp.clip(with_spikes(result, jax.random.fold_in(own_key, 3), *heavy), -limit, limit).astype(kind)


def setup_inputs(seed: int = 0) -> dict:
    seeds = jax.random.split(jax.random.key(seed), 7)
    tokens = bell_draw_with(seeds[0], (TOKENS, D), 1.0, 24.0, ((0, 512),), (0, 1, 512, 6.0))
    out_grad = bell_draw_with(seeds[1], (TOKENS, D), 1.0, 24.0, ((0, 512),), (0, 1, 512, 6.0))
    up_codes = jnp.clip(jax.random.uniform(seeds[2], (D, BUCKET), jnp.float32, -127.0, 127.0) * levels(seeds[2], (D, BUCKET), ((0, 8),), -0.4, 0.0), -127.0, 127.0).astype(jnp.bfloat16)
    up_scales = jnp.clip(jnp.exp(math.log(0.0004375) - 1.3862944 * jax.random.uniform(seeds[3], (D, NBLOCK), jnp.float32) ** levels(seeds[3], (D, NBLOCK), ((0, 8),), -0.2, 0.2)), 0.000109375, 0.0004375)
    down_codes = jnp.clip(jax.random.uniform(seeds[4], (D, BUCKET), jnp.float32, -127.0, 127.0) * levels(seeds[4], (D, BUCKET), ((0, 8),), -0.4, 0.0), -127.0, 127.0).astype(jnp.bfloat16)
    down_scales = jnp.clip(jnp.exp(math.log(0.0004375) - 1.3862944 * jax.random.uniform(seeds[5], (D, NBLOCK), jnp.float32) ** levels(seeds[5], (D, NBLOCK), ((0, 8),), -0.2, 0.2)), 0.000109375, 0.0004375)
    return {"tokens": tokens, "out_grad": out_grad, "up_codes": up_codes, "up_scales": up_scales, "down_codes": down_codes, "down_scales": down_scales}


def gelu_tanh(values):
    return jax.nn.gelu(values, approximate=True)

def quantize(values):
    blocks = values.reshape(values.shape[:-1] + (values.shape[-1] // QBLOCK, QBLOCK))
    scales = 2.0 * jnp.sqrt(lax.optimization_barrier(jnp.mean(blocks * blocks, axis=-1)) + 1e-06) / 7.0
    block_codes = jnp.clip(blocks / scales[..., None], -7.0, 7.0).astype(jnp.bfloat16).reshape(values.shape)
    return (block_codes, scales)

def restore(block_codes, scales):
    blocks = block_codes.astype(jnp.float32).reshape(block_codes.shape[:-1] + (scales.shape[-1], -1))
    return (blocks * scales[..., None]).reshape(block_codes.shape)

def reference(tokens, out_grad, up_codes, up_scales, down_codes, down_scales):
    up = restore(up_codes, up_scales).astype(jnp.bfloat16)
    down = restore(down_codes, down_scales).astype(jnp.bfloat16)
    preact = jnp.dot(tokens, up, preferred_element_type=jnp.float32)
    activated, slope_fn = jax.vjp(gelu_tanh, preact)
    activated = activated.astype(jnp.bfloat16)
    back_grad = jnp.dot(out_grad, down, preferred_element_type=jnp.float32)
    hidden_grad = slope_fn(back_grad)[0].astype(jnp.bfloat16)
    input_grad = jnp.dot(hidden_grad, up.T, preferred_element_type=jnp.float32).astype(jnp.bfloat16)
    token_blocks = tokens.reshape(N_NODE, N_LOCAL, TOK_DEV, D)
    out_blocks = out_grad.reshape(N_NODE, N_LOCAL, TOK_DEV, D)
    hidden_blocks = hidden_grad.reshape(N_NODE, N_LOCAL, TOK_DEV, BUCKET)
    active_blocks = activated.reshape(N_NODE, N_LOCAL, TOK_DEV, BUCKET)

    def device_term(inner):
        inputs, outs, hiddens, actives = inner
        first = jnp.dot(inputs.T, hiddens, preferred_element_type=jnp.float32)
        second = jnp.dot(outs.T, actives, preferred_element_type=jnp.float32)
        block_codes, scales = quantize(jnp.stack([first, second]))
        return restore(block_codes, scales)

    def node_step(carry, node_items):
        summed = lax.optimization_barrier(jnp.sum(lax.map(device_term, node_items), axis=0))
        block_codes, scales = quantize(summed)
        return (carry + restore(block_codes, scales), None)
    total, _ = lax.scan(node_step, jnp.zeros((2, D, BUCKET), jnp.float32), (token_blocks, out_blocks, hidden_blocks, active_blocks))
    total = total / (N_NODE * N_LOCAL)
    return (input_grad, total[0], total[1])
```

```python
import functools
import math
import jax
import jax.numpy as jnp
from jax import lax
from jax.experimental import pallas as pl
from jax.experimental.pallas import tpu as pltpu
from jax.sharding import Mesh, PartitionSpec as P

QBLOCK = 128
AXES = ("yh", "z", "c", "x", "yl")
LOCAL = ("x", "yl")
GROUP = ("z", "c")
VMEM_LIMIT = 40 * 1024 * 1024


def exchange(array, axes):
    return lax.all_to_all(array, axes, split_axis=0, concat_axis=0, tiled=True)


def clip_blocks(values):
    parts = []
    for k in range(values.shape[1] // QBLOCK):
        block = values[:, k * QBLOCK : (k + 1) * QBLOCK]
        mean = jnp.mean(block * block, axis=-1, keepdims=True)
        scale = 2.0 * jnp.sqrt(mean + 1e-06) / 7.0
        codes = jnp.clip(block * (1.0 / scale), -7.0, 7.0).astype(jnp.bfloat16)
        parts.append(codes.astype(jnp.float32) * scale)
    return jnp.concatenate(parts, axis=1)


def inner_tanh(v):
    return jnp.tanh(math.sqrt(2.0 / math.pi) * (v + 0.044715 * v * v * v))


def forward_kernel(weights_ref, tokens_ref, preact_ref, act_ref, up_ref, total):
    step = pl.program_id(0)

    @pl.when(step == 0)
    def _():
        total[...] = jnp.zeros_like(total)

    w = weights_ref[...].reshape(-1, weights_ref.shape[-1]).astype(jnp.bfloat16)
    up_ref[...] = w
    total[...] += jnp.dot(tokens_ref[...], w, preferred_element_type=jnp.float32)

    @pl.when(step == pl.num_programs(0) - 1)
    def _():
        v = total[...]
        preact_ref[...] = v
        act = 0.5 * v * (1.0 + inner_tanh(v))
        act_ref[...] = act.astype(jnp.bfloat16).astype(jnp.float32)


def backward_kernel(weights_ref, grads_ref, preact_ref, hidden_ref, total):
    step = pl.program_id(0)

    @pl.when(step == 0)
    def _():
        total[...] = jnp.zeros_like(total)

    w = weights_ref[...].reshape(-1, weights_ref.shape[-1]).astype(jnp.bfloat16)
    total[...] += jnp.dot(grads_ref[...], w, preferred_element_type=jnp.float32)

    @pl.when(step == pl.num_programs(0) - 1)
    def _():
        v = preact_ref[...]
        t = inner_tanh(v)
        slope = 0.5 * (1.0 + t) + 0.5 * v * (1.0 - t * t) * math.sqrt(2.0 / math.pi) * (
            1.0 + 3.0 * 0.044715 * v * v
        )
        hidden_ref[...] = (total[...] * slope).astype(jnp.bfloat16).astype(jnp.float32)


def weight_spec(shape):
    return pl.BlockSpec((shape[0], None, shape[2], shape[3]), lambda k: (0, k, 0, 0))


def forward(weights, tokens):
    groups, n, piece, width = weights.shape
    rows, depth = tokens.shape
    whole = pl.BlockSpec((rows, width), lambda k: (0, 0))
    return pl.pallas_call(
        forward_kernel,
        grid=(n,),
        in_specs=[weight_spec(weights.shape), pl.BlockSpec((rows, depth // n), lambda k: (0, k))],
        out_specs=[whole, whole, pl.BlockSpec((depth // n, width), lambda k: (k, 0))],
        out_shape=[
            jax.ShapeDtypeStruct((rows, width), jnp.float32),
            jax.ShapeDtypeStruct((rows, width), jnp.float32),
            jax.ShapeDtypeStruct((depth, width), jnp.bfloat16),
        ],
        scratch_shapes=[pltpu.VMEM((rows, width), jnp.float32)],
        compiler_params=pltpu.CompilerParams(vmem_limit_bytes=VMEM_LIMIT),
        cost_estimate=pl.CostEstimate(
            flops=2 * rows * depth * width, bytes_accessed=8000000, transcendentals=rows * width
        ),
        name="forward",
    )(weights, tokens)


def backward(weights, grads, preact):
    groups, n, piece, width = weights.shape
    rows, depth = grads.shape
    whole = pl.BlockSpec((rows, width), lambda k: (0, 0))
    return pl.pallas_call(
        backward_kernel,
        grid=(n,),
        in_specs=[
            weight_spec(weights.shape),
            pl.BlockSpec((rows, depth // n), lambda k: (0, k)),
            whole,
        ],
        out_specs=whole,
        out_shape=jax.ShapeDtypeStruct((rows, width), jnp.float32),
        scratch_shapes=[pltpu.VMEM((rows, width), jnp.float32)],
        compiler_params=pltpu.CompilerParams(vmem_limit_bytes=VMEM_LIMIT),
        cost_estimate=pl.CostEstimate(
            flops=2 * rows * depth * width, bytes_accessed=6000000, transcendentals=rows * width
        ),
        name="backward",
    )(weights, grads, preact)


def node_kernel(core_ref, left_ref, right_ref, mine_ref, other_ref, total):
    step = pl.program_id(0)

    @pl.when(step == 0)
    def _():
        total[...] = jnp.zeros_like(total)

    term = lax.dot_general(
        left_ref[...].astype(jnp.bfloat16),
        right_ref[...].astype(jnp.bfloat16),
        (((0,), (0,)), ((), ())),
        preferred_element_type=jnp.float32,
    )
    total[...] += clip_blocks(term)

    @pl.when(step == pl.num_programs(0) - 1)
    def _():
        pairs, rows, width = mine_ref.shape
        summed = clip_blocks(total[...]).reshape(pairs, 2, rows, width)
        first = core_ref[0] == 0
        mine_ref[...] = jnp.where(first, summed[:, 0], summed[:, 1])
        other_ref[...] = jnp.where(first, summed[:, 1], summed[:, 0])


def node_sum(core, left, right, owned):
    n, rows, height = left.shape
    width = right.shape[2]
    half = (height // (2 * owned), owned, width)
    out = pl.BlockSpec(half, lambda k, core_ref: (0, 0, 0))
    return pl.pallas_call(
        node_kernel,
        grid_spec=pltpu.PrefetchScalarGridSpec(
            num_scalar_prefetch=1,
            grid=(n,),
            in_specs=[
                pl.BlockSpec((None, rows, height), lambda k, core_ref: (k, 0, 0)),
                pl.BlockSpec((None, rows, width), lambda k, core_ref: (k, 0, 0)),
            ],
            out_specs=[out, out],
            scratch_shapes=[pltpu.VMEM((height, width), jnp.float32)],
        ),
        out_shape=[jax.ShapeDtypeStruct(half, jnp.float32)] * 2,
        compiler_params=pltpu.CompilerParams(vmem_limit_bytes=VMEM_LIMIT),
        cost_estimate=pl.CostEstimate(
            flops=2 * n * rows * height * width, bytes_accessed=5000000, transcendentals=0
        ),
        name="node_sum",
    )(core, left, right)


def local(tokens, out_grad, up_codes, up_scales, down_codes, down_scales):
    n_local = lax.axis_size(LOCAL)
    n_group = lax.axis_size(GROUP)
    devices_all = lax.axis_size(AXES)
    rows, depth = tokens.shape
    shard, width = up_codes.shape
    owned = depth // devices_all
    core = lax.axis_index("c")

    def product(codes, scales):
        piece = shard // n_group
        start = lax.axis_index(GROUP) * piece
        own = lax.dynamic_slice_in_dim(codes, start, piece, 0).astype(jnp.float32)
        own_scales = lax.dynamic_slice_in_dim(scales, start, piece, 0)
        return own * jnp.repeat(own_scales, QBLOCK, axis=1)

    def by_slices(array):
        cut = array.reshape(rows, n_local, depth // n_local).transpose(1, 0, 2)
        return cut.astype(jnp.float32)

    def to_all(array):
        return exchange(jnp.broadcast_to(array[None], (n_local,) + array.shape), LOCAL)

    pieces = to_all(jnp.stack([product(up_codes, up_scales), product(down_codes, down_scales)]))
    up_all = lax.all_gather(pieces[:, 0], GROUP, axis=0)
    down_all = lax.all_gather(pieces[:, 1], GROUP, axis=0)
    grads_cut = exchange(by_slices(out_grad), LOCAL)
    preact, activated, up = forward(up_all, tokens)
    activated_all = to_all(activated)
    tokens_cut = exchange(by_slices(tokens), LOCAL)

    def finish(left, right):
        mine, other = node_sum(core[None], left, right, owned)
        both = mine + lax.ppermute(other, "c", [(0, 1), (1, 0)])
        return jnp.sum(exchange(both, ("yh", "z")), axis=0) / devices_all

    grad_down = finish(grads_cut, activated_all)
    hidden = backward(down_all, out_grad, preact)
    hidden_all = to_all(hidden)
    input_grad = lax.dot_general(
        hidden.astype(jnp.bfloat16), up, (((1,), (1,)), ((), ())), preferred_element_type=jnp.float32
    ).astype(jnp.bfloat16)
    grad_up = finish(tokens_cut, hidden_all)
    return (input_grad, grad_up, grad_down)


def solution(mesh):
    fine = Mesh(mesh.devices.reshape(4, 8, 2, 4, 2), AXES)
    by_tokens = P(AXES, None)
    by_rows = P(LOCAL, None)
    owned_rows = P(LOCAL + ("yh", "z", "c"), None)
    return jax.shard_map(
        local,
        mesh=fine,
        in_specs=(by_tokens, by_tokens, by_rows, by_rows, by_rows, by_rows),
        out_specs=(by_tokens, owned_rows, owned_rows),
        check_vma=False,
    )
```

```python
import functools
import math
import jax
import jax.numpy as jnp
from jax import lax
from jax.experimental import pallas as pl
from jax.experimental.pallas import tpu as pltpu
from jax.sharding import Mesh, PartitionSpec as P

QBLOCK = 128
AXES = ("yh", "z", "c", "x", "yl")
LOCAL = ("x", "yl")
GROUP = ("z", "c")
VMEM_LIMIT = 40 * 1024 * 1024


def exchange(array, axes):
    return lax.all_to_all(array, axes, split_axis=0, concat_axis=0, tiled=True)


def clip_blocks(values):
    parts = []
    for k in range(values.shape[1] // QBLOCK):
        block = values[:, k * QBLOCK : (k + 1) * QBLOCK]
        mean = jnp.mean(block * block, axis=-1, keepdims=True)
        scale = 2.0 * jnp.sqrt(mean + 1e-06) / 7.0
        codes = jnp.clip(block * (1.0 / scale), -7.0, 7.0).astype(jnp.bfloat16)
        parts.append(codes.astype(jnp.float32) * scale)
    return jnp.concatenate(parts, axis=1)


def inner_tanh(v):
    return jnp.tanh(math.sqrt(2.0 / math.pi) * (v + 0.044715 * v * v * v))


def hidden_kernel(up_ref, down_ref, tokens_ref, grads_ref, act_ref, hidden_ref, upw_ref, pre, back):
    step = pl.program_id(0)

    @pl.when(step == 0)
    def _():
        pre[...] = jnp.zeros_like(pre)
        back[...] = jnp.zeros_like(back)

    width = up_ref.shape[-1]
    up = up_ref[...].reshape(-1, width).astype(jnp.bfloat16)
    down = down_ref[...].reshape(-1, width).astype(jnp.bfloat16)
    upw_ref[...] = up
    pre[...] += jnp.dot(tokens_ref[...], up, preferred_element_type=jnp.float32)
    back[...] += jnp.dot(grads_ref[...], down, preferred_element_type=jnp.float32)

    @pl.when(step == pl.num_programs(0) - 1)
    def _():
        v = pre[...]
        t = inner_tanh(v)
        act_ref[...] = (0.5 * v * (1.0 + t)).astype(jnp.bfloat16).astype(jnp.float32)
        slope = 0.5 * (1.0 + t) + 0.5 * v * (1.0 - t * t) * math.sqrt(2.0 / math.pi) * (
            1.0 + 3.0 * 0.044715 * v * v
        )
        hidden_ref[...] = (back[...] * slope).astype(jnp.bfloat16).astype(jnp.float32)


def hidden_pass(weights, tokens, grads):
    groups, n, _, piece, width = weights.shape
    rows, depth = tokens.shape
    whole = pl.BlockSpec((rows, width), lambda k: (0, 0))
    block = (groups, None, None, piece, width)
    cut = pl.BlockSpec((rows, depth // n), lambda k: (0, k))
    return pl.pallas_call(
        hidden_kernel,
        grid=(n,),
        in_specs=[
            pl.BlockSpec(block, lambda k: (0, k, 0, 0, 0)),
            pl.BlockSpec(block, lambda k: (0, k, 1, 0, 0)),
            cut,
            cut,
        ],
        out_specs=[whole, whole, pl.BlockSpec((depth // n, width), lambda k: (k, 0))],
        out_shape=[
            jax.ShapeDtypeStruct((rows, width), jnp.float32),
            jax.ShapeDtypeStruct((rows, width), jnp.float32),
            jax.ShapeDtypeStruct((depth, width), jnp.bfloat16),
        ],
        scratch_shapes=[pltpu.VMEM((rows, width), jnp.float32)] * 2,
        compiler_params=pltpu.CompilerParams(vmem_limit_bytes=VMEM_LIMIT),
        cost_estimate=pl.CostEstimate(
            flops=4 * rows * depth * width, bytes_accessed=13000000, transcendentals=rows * width
        ),
        name="hidden_pass",
    )(weights, weights, tokens, grads)


def cut_kernel(tokens_ref, grads_ref, out_ref):
    rows = tokens_ref.shape[0]
    out_ref[:rows] = tokens_ref[...].astype(jnp.float32)
    out_ref[rows:] = grads_ref[...].astype(jnp.float32)


def cut_columns(tokens, grads, n):
    rows, depth = tokens.shape
    cut = pl.BlockSpec((rows, depth // n), lambda k: (0, k))
    return pl.pallas_call(
        cut_kernel,
        grid=(n,),
        in_specs=[cut, cut],
        out_specs=pl.BlockSpec((None, 2 * rows, depth // n), lambda k: (k, 0, 0)),
        out_shape=jax.ShapeDtypeStruct((n, 2 * rows, depth // n), jnp.float32),
        compiler_params=pltpu.CompilerParams(vmem_limit_bytes=VMEM_LIMIT),
        cost_estimate=pl.CostEstimate(flops=0, bytes_accessed=8000000, transcendentals=0),
        name="cut_columns",
    )(tokens, grads)


def node_kernel(core_ref, left_ref, right_ref, mine_ref, other_ref, total):
    step = pl.program_id(0)

    @pl.when(step == 0)
    def _():
        total[...] = jnp.zeros_like(total)

    term = lax.dot_general(
        left_ref[...].astype(jnp.bfloat16),
        right_ref[...].astype(jnp.bfloat16),
        (((0,), (0,)), ((), ())),
        preferred_element_type=jnp.float32,
    )
    total[...] += clip_blocks(term)

    @pl.when(step == pl.num_programs(0) - 1)
    def _():
        pairs, rows, width = mine_ref.shape
        summed = clip_blocks(total[...]).reshape(pairs, 2, rows, width)
        first = core_ref[0] == 0
        mine_ref[...] = jnp.where(first, summed[:, 0], summed[:, 1])
        other_ref[...] = jnp.where(first, summed[:, 1], summed[:, 0])


def node_sum(core, left, which, right, owned):
    height = left.shape[2]
    n, rows, width = right.shape
    half = (height // (2 * owned), owned, width)
    out = pl.BlockSpec(half, lambda k, core_ref: (0, 0, 0))
    return pl.pallas_call(
        node_kernel,
        grid_spec=pltpu.PrefetchScalarGridSpec(
            num_scalar_prefetch=1,
            grid=(n,),
            in_specs=[
                pl.BlockSpec((None, rows, height), lambda k, core_ref: (k, which, 0)),
                pl.BlockSpec((None, rows, width), lambda k, core_ref: (k, 0, 0)),
            ],
            out_specs=[out, out],
            scratch_shapes=[pltpu.VMEM((height, width), jnp.float32)],
        ),
        out_shape=[jax.ShapeDtypeStruct(half, jnp.float32)] * 2,
        compiler_params=pltpu.CompilerParams(vmem_limit_bytes=VMEM_LIMIT),
        cost_estimate=pl.CostEstimate(
            flops=2 * n * rows * height * width, bytes_accessed=5000000, transcendentals=0
        ),
        name="node_sum",
    )(core, left, right)


def local(tokens, out_grad, up_codes, up_scales, down_codes, down_scales):
    n_local = lax.axis_size(LOCAL)
    n_group = lax.axis_size(GROUP)
    devices_all = lax.axis_size(AXES)
    rows, depth = tokens.shape
    shard, width = up_codes.shape
    owned = depth // devices_all
    core = lax.axis_index("c")

    def product(codes, scales):
        piece = shard // n_group
        start = lax.axis_index(GROUP) * piece
        own = lax.dynamic_slice_in_dim(codes, start, piece, 0).astype(jnp.float32)
        own_scales = lax.dynamic_slice_in_dim(scales, start, piece, 0)
        return own * jnp.repeat(own_scales, QBLOCK, axis=1)

    def to_all(array):
        return exchange(jnp.broadcast_to(array[None], (n_local,) + array.shape), LOCAL)

    pieces = to_all(jnp.stack([product(up_codes, up_scales), product(down_codes, down_scales)]))
    weights = lax.all_gather(pieces, GROUP, axis=0)
    columns = exchange(cut_columns(tokens, out_grad, n_local), LOCAL)
    activated, hidden, up = hidden_pass(weights, tokens, out_grad)

    def over_cores(which, right):
        mine, other = node_sum(core[None], columns, which, right, owned)
        return mine + lax.ppermute(other, "c", [(0, 1), (1, 0)])

    activated_all = to_all(activated)
    hidden_all = to_all(hidden)
    grad_down = over_cores(1, activated_all)
    grad_up = over_cores(0, hidden_all)
    input_grad = lax.dot_general(
        hidden.astype(jnp.bfloat16), up, (((1,), (1,)), ((), ())), preferred_element_type=jnp.float32
    ).astype(jnp.bfloat16)
    owned_sums = exchange(jnp.concatenate([grad_up, grad_down], axis=1), ("yh", "z"))
    grads = jnp.sum(owned_sums, axis=0) / devices_all
    return (input_grad, grads[:owned], grads[owned:])


def solution(mesh):
    fine = Mesh(mesh.devices.reshape(4, 8, 2, 4, 2), AXES)
    by_tokens = P(AXES, None)
    by_rows = P(LOCAL, None)
    owned_rows = P(LOCAL + ("yh", "z", "c"), None)
    return jax.shard_map(
        local,
        mesh=fine,
        in_specs=(by_tokens, by_tokens, by_rows, by_rows, by_rows, by_rows),
        out_specs=(by_tokens, owned_rows, owned_rows),
        check_vma=False,
    )
```

```python
import functools
import math
import jax
import jax.numpy as jnp
from jax import lax
from jax.experimental import pallas as pl
from jax.experimental.pallas import tpu as pltpu
from jax.sharding import Mesh, PartitionSpec as P

QBLOCK = 128
AXES = ("yh", "z", "c", "x", "yl")
LOCAL = ("x", "yl")
GROUP = ("z", "c")
VMEM_LIMIT = 56 * 1024 * 1024


def exchange(array, axes):
    return lax.all_to_all(array, axes, split_axis=0, concat_axis=0, tiled=True)


def clip_blocks(values, averages):
    squares = values * values
    high = squares.astype(jnp.bfloat16)
    low = (squares - high.astype(jnp.float32)).astype(jnp.bfloat16)
    mean = jnp.dot(high, averages, preferred_element_type=jnp.float32)
    mean += jnp.dot(low, averages, preferred_element_type=jnp.float32)
    mean += 1e-06
    root = lax.rsqrt(mean)
    codes = jnp.clip(values * (3.5 * root), -7.0, 7.0).astype(jnp.bfloat16)
    return codes.astype(jnp.float32) * (mean * root * (2.0 / 7.0))


def block_averages(width):
    rows = lax.broadcasted_iota(jnp.int32, (width, width), 0) // QBLOCK
    columns = lax.broadcasted_iota(jnp.int32, (width, width), 1) // QBLOCK
    return jnp.where(rows == columns, 1.0 / QBLOCK, 0.0).astype(jnp.bfloat16)


def inner_tanh(v):
    return jnp.tanh(math.sqrt(2.0 / math.pi) * (v + 0.044715 * v * v * v))


def hidden_kernel(up_ref, down_ref, tokens_ref, grads_ref, both_ref, upw_ref, pre, back):
    step = pl.program_id(0)

    @pl.when(step == 0)
    def _():
        pre[...] = jnp.zeros_like(pre)
        back[...] = jnp.zeros_like(back)

    width = up_ref.shape[-1]
    up = up_ref[...].reshape(-1, width).astype(jnp.bfloat16)
    down = down_ref[...].reshape(-1, width).astype(jnp.bfloat16)
    upw_ref[...] = up
    pre[...] += jnp.dot(tokens_ref[...], up, preferred_element_type=jnp.float32)
    back[...] += jnp.dot(grads_ref[...], down, preferred_element_type=jnp.float32)

    @pl.when(step == pl.num_programs(0) - 1)
    def _():
        v = pre[...]
        t = inner_tanh(v)
        act = (0.5 * v * (1.0 + t)).astype(jnp.bfloat16).astype(jnp.float32)
        slope = 0.5 * (1.0 + t) + 0.5 * v * (1.0 - t * t) * math.sqrt(2.0 / math.pi) * (
            1.0 + 3.0 * 0.044715 * v * v
        )
        hidden = (back[...] * slope).astype(jnp.bfloat16).astype(jnp.float32)
        for k in range(both_ref.shape[0]):
            both_ref[k, 0] = hidden
            both_ref[k, 1] = act


def hidden_pass(weights, tokens, grads):
    groups, n, _, piece, width = weights.shape
    rows, depth = tokens.shape
    block = (groups, None, None, piece, width)
    cut = pl.BlockSpec((rows, depth // n), lambda k: (0, k))
    return pl.pallas_call(
        hidden_kernel,
        grid=(n,),
        in_specs=[
            pl.BlockSpec(block, lambda k: (0, k, 0, 0, 0)),
            pl.BlockSpec(block, lambda k: (0, k, 1, 0, 0)),
            cut,
            cut,
        ],
        out_specs=[
            pl.BlockSpec((n, 2, rows, width), lambda k: (0, 0, 0, 0)),
            pl.BlockSpec((depth // n, width), lambda k: (k, 0)),
        ],
        out_shape=[
            jax.ShapeDtypeStruct((n, 2, rows, width), jnp.float32),
            jax.ShapeDtypeStruct((depth, width), jnp.bfloat16),
        ],
        scratch_shapes=[pltpu.VMEM((rows, width), jnp.float32)] * 2,
        compiler_params=pltpu.CompilerParams(vmem_limit_bytes=VMEM_LIMIT),
        cost_estimate=pl.CostEstimate(
            flops=4 * rows * depth * width, bytes_accessed=13000000, transcendentals=rows * width
        ),
        name="hidden_pass",
    )(weights, weights, tokens, grads)


def cut_kernel(tokens_ref, grads_ref, out_ref):
    rows = tokens_ref.shape[0]
    out_ref[:rows] = tokens_ref[...].astype(jnp.float32)
    out_ref[rows:] = grads_ref[...].astype(jnp.float32)


def cut_columns(tokens, grads, n):
    rows, depth = tokens.shape
    cut = pl.BlockSpec((rows, depth // n), lambda k: (0, k))
    return pl.pallas_call(
        cut_kernel,
        grid=(n,),
        in_specs=[cut, cut],
        out_specs=pl.BlockSpec((None, 2 * rows, depth // n), lambda k: (k, 0, 0)),
        out_shape=jax.ShapeDtypeStruct((n, 2 * rows, depth // n), jnp.float32),
        compiler_params=pltpu.CompilerParams(vmem_limit_bytes=VMEM_LIMIT),
        cost_estimate=pl.CostEstimate(flops=0, bytes_accessed=8000000, transcendentals=0),
        name="cut_columns",
    )(tokens, grads)


def node_kernel(core_ref, left_ref, right_ref, mine_ref, other_ref, total):
    step = pl.program_id(0)

    @pl.when(step == 0)
    def _():
        total[...] = jnp.zeros_like(total)

    term = lax.dot_general(
        left_ref[...].astype(jnp.bfloat16),
        right_ref[...].astype(jnp.bfloat16),
        (((0,), (0,)), ((), ())),
        preferred_element_type=jnp.float32,
    )
    averages = block_averages(term.shape[1])
    total[...] += clip_blocks(term, averages)

    @pl.when(step == pl.num_programs(0) - 1)
    def _():
        pairs, rows, width = mine_ref.shape
        summed = clip_blocks(total[...], averages).reshape(pairs, 2, rows, width)
        first = core_ref[0] == 0
        mine_ref[...] = jnp.where(first, summed[:, 0], summed[:, 1])
        other_ref[...] = jnp.where(first, summed[:, 1], summed[:, 0])


def node_sum(core, left, which, right, owned):
    height = left.shape[2]
    n, _, rows, width = right.shape
    half = (height // (2 * owned), owned, width)
    out = pl.BlockSpec(half, lambda k, core_ref: (0, 0, 0))
    return pl.pallas_call(
        node_kernel,
        grid_spec=pltpu.PrefetchScalarGridSpec(
            num_scalar_prefetch=1,
            grid=(n,),
            in_specs=[
                pl.BlockSpec((None, rows, height), lambda k, core_ref: (k, which, 0)),
                pl.BlockSpec((None, None, rows, width), lambda k, core_ref: (k, which, 0, 0)),
            ],
            out_specs=[out, out],
            scratch_shapes=[pltpu.VMEM((height, width), jnp.float32)],
        ),
        out_shape=[jax.ShapeDtypeStruct(half, jnp.float32)] * 2,
        compiler_params=pltpu.CompilerParams(vmem_limit_bytes=VMEM_LIMIT),
        cost_estimate=pl.CostEstimate(
            flops=2 * n * rows * height * width, bytes_accessed=5000000, transcendentals=0
        ),
        name="node_sum",
    )(core, left, right)


def local(tokens, out_grad, up_codes, up_scales, down_codes, down_scales):
    n_local = lax.axis_size(LOCAL)
    n_group = lax.axis_size(GROUP)
    devices_all = lax.axis_size(AXES)
    rows, depth = tokens.shape
    shard, width = up_codes.shape
    owned = depth // devices_all
    core = lax.axis_index("c")

    def product(codes, scales):
        piece = shard // n_group
        start = lax.axis_index(GROUP) * piece
        own = lax.dynamic_slice_in_dim(codes, start, piece, 0).astype(jnp.float32)
        own_scales = lax.dynamic_slice_in_dim(scales, start, piece, 0)
        return own * jnp.repeat(own_scales, QBLOCK, axis=1)

    def to_all(array):
        return exchange(jnp.broadcast_to(array[None], (n_local,) + array.shape), LOCAL)

    pieces = to_all(jnp.stack([product(up_codes, up_scales), product(down_codes, down_scales)]))
    pieces, cut = lax.optimization_barrier((pieces, cut_columns(tokens, out_grad, n_local)))
    weights = lax.all_gather(pieces, GROUP, axis=0)
    columns = exchange(cut, LOCAL)
    both, up = hidden_pass(weights, tokens, out_grad)
    hidden = both[0, 0]
    both_all = exchange(both, LOCAL)

    def over_cores(which):
        mine, other = node_sum(core[None], columns, which, both_all, owned)
        return mine + lax.ppermute(other, "c", [(0, 1), (1, 0)])

    grad_down = over_cores(1)
    grad_up = over_cores(0)
    input_grad = lax.dot_general(
        hidden.astype(jnp.bfloat16), up, (((1,), (1,)), ((), ())), preferred_element_type=jnp.float32
    ).astype(jnp.bfloat16)
    owned_sums = exchange(jnp.concatenate([grad_up, grad_down], axis=1), ("yh", "z"))
    grads = jnp.sum(owned_sums, axis=0) / devices_all
    return (input_grad, grads[:owned], grads[owned:])


def solution(mesh):
    fine = Mesh(mesh.devices.reshape(4, 8, 2, 4, 2), AXES)
    by_tokens = P(AXES, None)
    by_rows = P(LOCAL, None)
    owned_rows = P(LOCAL + ("yh", "z", "c"), None)
    return jax.shard_map(
        local,
        mesh=fine,
        in_specs=(by_tokens, by_tokens, by_rows, by_rows, by_rows, by_rows),
        out_specs=(by_tokens, owned_rows, owned_rows),
        check_vma=False,
    )
```

```python
import functools
import math
import jax
import jax.numpy as jnp
from jax import lax
from jax.experimental import pallas as pl
from jax.experimental.pallas import tpu as pltpu
from jax.sharding import Mesh, PartitionSpec as P

QBLOCK = 128
AXES = ("yh", "z", "c", "x", "yl")
LOCAL = ("x", "yl")
GROUP = ("z", "c")
SHARDS = 2
VMEM_LIMIT = 16 * 1024 * 1024


def exchange(array, axes):
    return lax.all_to_all(array, axes, split_axis=0, concat_axis=0, tiled=True)


def clip_blocks(values):
    parts = []
    for k in range(values.shape[0] // QBLOCK):
        block = values[k * QBLOCK : (k + 1) * QBLOCK]
        mean = jnp.mean(block * block, axis=0, keepdims=True) + 1e-06
        root = lax.rsqrt(mean)
        codes = jnp.clip(block * (3.5 * root), -7.0, 7.0).astype(jnp.bfloat16)
        parts.append(codes.astype(jnp.float32) * (mean * root * (2.0 / 7.0)))
    return jnp.concatenate(parts, axis=0)


def inner_tanh(v):
    return jnp.tanh(math.sqrt(2.0 / math.pi) * (v + 0.044715 * v * v * v))


def hidden_kernel(weights_ref, tokens_ref, grads_ref, both_ref, pre, back):
    step = pl.program_id(0)

    @pl.when(step == 0)
    def _():
        pre[...] = jnp.zeros_like(pre)
        back[...] = jnp.zeros_like(back)

    _, shards, _, _, width = weights_ref.shape
    shard = tokens_ref.shape[1] // shards
    for q in range(shards):
        up = weights_ref[:, q, 0].reshape(shard, width).astype(jnp.bfloat16)
        down = weights_ref[:, q, 1].reshape(shard, width).astype(jnp.bfloat16)
        columns = slice(q * shard, (q + 1) * shard)
        pre[...] += jnp.dot(tokens_ref[:, columns], up, preferred_element_type=jnp.float32)
        back[...] += jnp.dot(grads_ref[:, columns], down, preferred_element_type=jnp.float32)

    @pl.when(step == pl.num_programs(0) - 1)
    def _():
        v = pre[...]
        t = inner_tanh(v)
        act = (0.5 * v * (1.0 + t)).astype(jnp.bfloat16).astype(jnp.float32)
        slope = 0.5 * (1.0 + t) + 0.5 * v * (1.0 - t * t) * math.sqrt(2.0 / math.pi) * (
            1.0 + 3.0 * 0.044715 * v * v
        )
        hidden = (back[...] * slope).astype(jnp.bfloat16).astype(jnp.float32)
        for k in range(both_ref.shape[0]):
            both_ref[k, 0] = hidden
            both_ref[k, 1] = act


def hidden_pass(weights, tokens, grads):
    groups, n, kinds, piece, width = weights.shape
    rows, depth = tokens.shape
    cut = pl.BlockSpec((rows, SHARDS * depth // n), lambda k: (0, k))
    return pl.pallas_call(
        hidden_kernel,
        grid=(n // SHARDS,),
        in_specs=[
            pl.BlockSpec((groups, SHARDS, kinds, piece, width), lambda k: (0, k, 0, 0, 0)),
            cut,
            cut,
        ],
        out_specs=pl.BlockSpec((n, 2, rows, width), lambda k: (0, 0, 0, 0)),
        out_shape=jax.ShapeDtypeStruct((n, 2, rows, width), jnp.float32),
        scratch_shapes=[pltpu.VMEM((rows, width), jnp.float32)] * 2,
        compiler_params=pltpu.CompilerParams(vmem_limit_bytes=VMEM_LIMIT),
        cost_estimate=pl.CostEstimate(
            flops=4 * rows * depth * width, bytes_accessed=13000000, transcendentals=rows * width
        ),
        name="hidden_pass",
    )(weights, tokens, grads)


def input_kernel(hidden_ref, weights_ref, out_ref):
    _, shards, _, width = weights_ref.shape
    shard = out_ref.shape[1] // shards
    hidden = hidden_ref[...].astype(jnp.bfloat16)
    for q in range(shards):
        up = weights_ref[:, q].reshape(shard, width).astype(jnp.bfloat16)
        out_ref[:, q * shard : (q + 1) * shard] = lax.dot_general(
            hidden, up, (((1,), (1,)), ((), ())), preferred_element_type=jnp.float32
        ).astype(out_ref.dtype)


def input_pass(both, weights):
    groups, n, _, piece, width = weights.shape
    rows = both.shape[2]
    depth = groups * n * piece
    return pl.pallas_call(
        input_kernel,
        grid=(n // SHARDS,),
        in_specs=[
            pl.BlockSpec((None, None, rows, width), lambda k: (0, 0, 0, 0)),
            pl.BlockSpec((groups, SHARDS, None, piece, width), lambda k: (0, k, 0, 0, 0)),
        ],
        out_specs=pl.BlockSpec((rows, SHARDS * depth // n), lambda k: (0, k)),
        out_shape=jax.ShapeDtypeStruct((rows, depth), jnp.bfloat16),
        compiler_params=pltpu.CompilerParams(vmem_limit_bytes=VMEM_LIMIT),
        cost_estimate=pl.CostEstimate(
            flops=2 * rows * depth * width, bytes_accessed=6000000, transcendentals=0
        ),
        name="input_pass",
    )(both, weights)


def piece_kernel(place_ref, up_ref, up_scales_ref, down_ref, down_scales_ref, out_ref):
    piece, width = up_ref.shape
    shard = up_scales_ref.shape[1]
    shape = (piece, shard)
    wanted = lax.broadcasted_iota(jnp.int32, shape, 0) + place_ref[0] * piece
    chosen = wanted == lax.broadcasted_iota(jnp.int32, shape, 1)
    for kind, (codes, scales) in enumerate(((up_ref, up_scales_ref), (down_ref, down_scales_ref))):
        for k in range(width // QBLOCK):
            own = jnp.sum(jnp.where(chosen, scales[k : k + 1], 0.0), axis=1, keepdims=True)
            columns = slice(k * QBLOCK, (k + 1) * QBLOCK)
            product = codes[:, columns].astype(jnp.float32) * own
            for p in range(out_ref.shape[0]):
                out_ref[p, kind, :, columns] = product


def make_pieces(place, n_group, n_local, up_codes, up_scales, down_codes, down_scales):
    shard, width = up_codes.shape
    piece = shard // n_group
    codes = pl.BlockSpec((piece, width), lambda k, place_ref: (place_ref[0], 0))
    scales = pl.BlockSpec(up_scales.T.shape, lambda k, place_ref: (0, 0))
    out = (n_local, 2, piece, width)
    return pl.pallas_call(
        piece_kernel,
        grid_spec=pltpu.PrefetchScalarGridSpec(
            num_scalar_prefetch=1,
            grid=(1,),
            in_specs=[codes, scales, codes, scales],
            out_specs=pl.BlockSpec(out, lambda k, place_ref: (0, 0, 0, 0)),
        ),
        out_shape=jax.ShapeDtypeStruct(out, jnp.float32),
        compiler_params=pltpu.CompilerParams(vmem_limit_bytes=VMEM_LIMIT),
        name="make_pieces",
    )(place[None], up_codes, up_scales.T, down_codes, down_scales.T)


def narrow_kernel(columns_ref, out_ref):
    out_ref[...] = columns_ref[...].astype(out_ref.dtype)


def narrow(columns):
    n = columns.shape[0]
    block = pl.BlockSpec((n // 2,) + columns.shape[1:], lambda k: (k, 0, 0))
    return pl.pallas_call(
        narrow_kernel,
        grid=(2,),
        in_specs=[block],
        out_specs=block,
        out_shape=jax.ShapeDtypeStruct(columns.shape, jnp.bfloat16),
        compiler_params=pltpu.CompilerParams(vmem_limit_bytes=VMEM_LIMIT),
        cost_estimate=pl.CostEstimate(flops=0, bytes_accessed=12000000, transcendentals=0),
        name="narrow",
    )(columns)


def cut_kernel(tokens_ref, grads_ref, out_ref):
    rows = tokens_ref.shape[0]
    out_ref[:rows] = tokens_ref[...].astype(jnp.float32)
    out_ref[rows:] = grads_ref[...].astype(jnp.float32)


def cut_columns(tokens, grads, n):
    rows, depth = tokens.shape
    cut = pl.BlockSpec((rows, depth // n), lambda k: (0, k))
    return pl.pallas_call(
        cut_kernel,
        grid=(n,),
        in_specs=[cut, cut],
        out_specs=pl.BlockSpec((None, 2 * rows, depth // n), lambda k: (k, 0, 0)),
        out_shape=jax.ShapeDtypeStruct((n, 2 * rows, depth // n), jnp.float32),
        compiler_params=pltpu.CompilerParams(vmem_limit_bytes=VMEM_LIMIT),
        cost_estimate=pl.CostEstimate(flops=0, bytes_accessed=8000000, transcendentals=0),
        name="cut_columns",
    )(tokens, grads)


def node_kernel(core_ref, left_ref, right_ref, mine_ref, other_ref):
    n, kinds, rows, _ = right_ref.shape
    owned = mine_ref.shape[1] // kinds
    for kind in range(kinds):
        total = None
        for p in range(n):
            term = lax.dot_general(
                right_ref[p, kind].astype(jnp.bfloat16),
                left_ref[p, kind * rows : (kind + 1) * rows],
                (((0,), (0,)), ((), ())),
                preferred_element_type=jnp.float32,
            )
            total = clip_blocks(term) if total is None else total + clip_blocks(term)
        summed = clip_blocks(total).T.reshape(mine_ref.shape[0], 2, owned, total.shape[0])
        first = core_ref[0] == 0
        part = slice(kind * owned, (kind + 1) * owned)
        mine_ref[:, part] = jnp.where(first, summed[:, 0], summed[:, 1])
        other_ref[:, part] = jnp.where(first, summed[:, 1], summed[:, 0])


def node_sums(core, left, right, owned):
    height = left.shape[2]
    n, kinds, rows, width = right.shape
    half = (height // (2 * owned), kinds * owned, width)
    out = pl.BlockSpec(half, lambda k, core_ref: (0, 0, 0))
    return pl.pallas_call(
        node_kernel,
        grid_spec=pltpu.PrefetchScalarGridSpec(
            num_scalar_prefetch=1,
            grid=(1,),
            in_specs=[
                pl.BlockSpec(left.shape, lambda k, core_ref: (0, 0, 0)),
                pl.BlockSpec(right.shape, lambda k, core_ref: (0, 0, 0, 0)),
            ],
            out_specs=[out, out],
        ),
        out_shape=[jax.ShapeDtypeStruct(half, jnp.float32)] * 2,
        compiler_params=pltpu.CompilerParams(vmem_limit_bytes=VMEM_LIMIT),
        cost_estimate=pl.CostEstimate(
            flops=4 * n * rows * height * width, bytes_accessed=9000000, transcendentals=0
        ),
        name="node_sums",
    )(core, left, right)


def local(tokens, out_grad, up_codes, up_scales, down_codes, down_scales):
    n_local = lax.axis_size(LOCAL)
    n_group = lax.axis_size(GROUP)
    devices_all = lax.axis_size(AXES)
    depth = tokens.shape[1]
    owned = depth // devices_all
    core = lax.axis_index("c")

    place = lax.axis_index(GROUP)
    pieces = exchange(
        make_pieces(place, n_group, n_local, up_codes, up_scales, down_codes, down_scales), LOCAL
    )
    pieces, cut = lax.optimization_barrier((pieces, cut_columns(tokens, out_grad, n_local)))
    weights = lax.all_gather(pieces, GROUP, axis=0)
    columns = exchange(cut, LOCAL)
    both = hidden_pass(weights, tokens, out_grad)
    both_all = exchange(both, LOCAL)

    mine, other = node_sums(core[None], narrow(columns), both_all, owned)
    input_grad = input_pass(both, weights)
    pairs = mine + lax.ppermute(other, "c", [(0, 1), (1, 0)])
    owned_sums = exchange(pairs, ("yh", "z"))
    grads = jnp.sum(owned_sums, axis=0) / devices_all
    return (input_grad, grads[:owned], grads[owned:])


def solution(mesh):
    fine = Mesh(mesh.devices.reshape(4, 8, 2, 4, 2), AXES)
    by_tokens = P(AXES, None)
    by_rows = P(LOCAL, None)
    owned_rows = P(LOCAL + ("yh", "z", "c"), None)
    return jax.shard_map(
        local,
        mesh=fine,
        in_specs=(by_tokens, by_tokens, by_rows, by_rows, by_rows, by_rows),
        out_specs=(by_tokens, owned_rows, owned_rows),
        check_vma=False,
    )
```

```python
import functools
import math
import jax
import jax.numpy as jnp
from jax import lax
from jax.experimental import pallas as pl
from jax.experimental.pallas import tpu as pltpu
from jax.sharding import Mesh, PartitionSpec as P

QBLOCK = 128
AXES = ("yh", "z", "c", "x", "yl")
LOCAL = ("x", "yl")
GROUP = ("z", "c")
SHARDS = 2
VMEM_LIMIT = 16 * 1024 * 1024
HIDDEN_LIMIT = 52 * 1024 * 1024
PIECE_LIMIT = 60 * 1024 * 1024


def exchange(array, axes):
    return lax.all_to_all(array, axes, split_axis=0, concat_axis=0, tiled=True)


def clip_blocks(values):
    parts = []
    for k in range(values.shape[0] // QBLOCK):
        block = values[k * QBLOCK : (k + 1) * QBLOCK]
        mean = jnp.mean(block * block, axis=0, keepdims=True) + 1e-06
        root = lax.rsqrt(mean)
        codes = jnp.clip(block * (3.5 * root), -7.0, 7.0).astype(jnp.bfloat16)
        parts.append(codes.astype(jnp.float32) * (mean * root * (2.0 / 7.0)))
    return jnp.concatenate(parts, axis=0)


def inner_tanh(v):
    return jnp.tanh(math.sqrt(2.0 / math.pi) * (v + 0.044715 * v * v * v))


def hidden_kernel(weights_hbm, tokens_ref, grads_ref, both_hbm, weights, both, pre, back, in_sems, out_sems):
    n, groups, _, piece, width = weights.shape
    shard = groups * piece
    arrivals = [
        pltpu.make_async_copy(weights_hbm.at[:, k], weights.at[k], in_sems.at[k]) for k in range(n)
    ]
    for copy in arrivals:
        copy.start()
    pre[...] = jnp.zeros_like(pre)
    back[...] = jnp.zeros_like(back)
    for k in range(n):
        arrivals[k].wait()
        up = weights[k, :, 0].reshape(shard, width).astype(jnp.bfloat16)
        down = weights[k, :, 1].reshape(shard, width).astype(jnp.bfloat16)
        columns = slice(k * shard, (k + 1) * shard)
        pre[...] += jnp.dot(tokens_ref[:, columns], up, preferred_element_type=jnp.float32)
        back[...] += jnp.dot(grads_ref[:, columns], down, preferred_element_type=jnp.float32)
    v = pre[...]
    t = inner_tanh(v)
    act = (0.5 * v * (1.0 + t)).astype(jnp.bfloat16).astype(jnp.float32)
    slope = 0.5 * (1.0 + t) + 0.5 * v * (1.0 - t * t) * math.sqrt(2.0 / math.pi) * (
        1.0 + 3.0 * 0.044715 * v * v
    )
    hidden = (back[...] * slope).astype(jnp.bfloat16).astype(jnp.float32)
    both[0] = hidden
    both[1] = act
    departures = [pltpu.make_async_copy(both, both_hbm.at[k], out_sems.at[k]) for k in range(n)]
    for copy in departures:
        copy.start()
    for copy in departures:
        copy.wait()


def hidden_pass(weights, tokens, grads):
    groups, n, kinds, piece, width = weights.shape
    rows, depth = tokens.shape
    return pl.pallas_call(
        hidden_kernel,
        in_specs=[
            pl.BlockSpec(memory_space=pltpu.HBM),
            pl.BlockSpec(memory_space=pltpu.VMEM),
            pl.BlockSpec(memory_space=pltpu.VMEM),
        ],
        out_specs=pl.BlockSpec(memory_space=pltpu.HBM),
        out_shape=jax.ShapeDtypeStruct((n, 2, rows, width), jnp.float32),
        scratch_shapes=[
            pltpu.VMEM((n, groups, kinds, piece, width), jnp.float32),
            pltpu.VMEM((2, rows, width), jnp.float32),
            pltpu.VMEM((rows, width), jnp.float32),
            pltpu.VMEM((rows, width), jnp.float32),
            pltpu.SemaphoreType.DMA((n,)),
            pltpu.SemaphoreType.DMA((n,)),
        ],
        compiler_params=pltpu.CompilerParams(vmem_limit_bytes=HIDDEN_LIMIT),
        cost_estimate=pl.CostEstimate(
            flops=4 * rows * depth * width, bytes_accessed=13000000, transcendentals=rows * width
        ),
        name="hidden_pass",
    )(weights, tokens, grads)


def input_kernel(hidden_ref, weights_ref, out_ref):
    _, shards, _, width = weights_ref.shape
    shard = out_ref.shape[1] // shards
    hidden = hidden_ref[...].astype(jnp.bfloat16)
    for q in range(shards):
        up = weights_ref[:, q].reshape(shard, width).astype(jnp.bfloat16)
        out_ref[:, q * shard : (q + 1) * shard] = lax.dot_general(
            hidden, up, (((1,), (1,)), ((), ())), preferred_element_type=jnp.float32
        ).astype(out_ref.dtype)


def input_pass(both, weights):
    groups, n, _, piece, width = weights.shape
    rows = both.shape[2]
    depth = groups * n * piece
    return pl.pallas_call(
        input_kernel,
        grid=(n // SHARDS,),
        in_specs=[
            pl.BlockSpec((None, None, rows, width), lambda k: (0, 0, 0, 0)),
            pl.BlockSpec((groups, SHARDS, None, piece, width), lambda k: (0, k, 0, 0, 0)),
        ],
        out_specs=pl.BlockSpec((rows, SHARDS * depth // n), lambda k: (0, k)),
        out_shape=jax.ShapeDtypeStruct((rows, depth), jnp.bfloat16),
        compiler_params=pltpu.CompilerParams(vmem_limit_bytes=VMEM_LIMIT),
        cost_estimate=pl.CostEstimate(
            flops=2 * rows * depth * width, bytes_accessed=6000000, transcendentals=0
        ),
        name="input_pass",
    )(both, weights)


def piece_kernel(place_ref, up_ref, up_scales_ref, down_ref, down_scales_ref, out_ref):
    piece, width = up_ref.shape
    shard = up_scales_ref.shape[1]
    shape = (piece, shard)
    wanted = lax.broadcasted_iota(jnp.int32, shape, 0) + place_ref[0] * piece
    chosen = wanted == lax.broadcasted_iota(jnp.int32, shape, 1)
    for kind, (codes, scales) in enumerate(((up_ref, up_scales_ref), (down_ref, down_scales_ref))):
        for k in range(width // QBLOCK):
            own = jnp.sum(jnp.where(chosen, scales[k : k + 1], 0.0), axis=1, keepdims=True)
            columns = slice(k * QBLOCK, (k + 1) * QBLOCK)
            product = codes[:, columns].astype(jnp.float32) * own
            for p in range(out_ref.shape[0]):
                out_ref[p, kind, :, columns] = product


def make_pieces(place, n_group, n_local, up_codes, up_scales, down_codes, down_scales):
    shard, width = up_codes.shape
    piece = shard // n_group
    codes = pl.BlockSpec((piece, width), lambda k, place_ref: (place_ref[0], 0))
    scales = pl.BlockSpec(up_scales.T.shape, lambda k, place_ref: (0, 0))
    out = (n_local, 2, piece, width)
    return pl.pallas_call(
        piece_kernel,
        grid_spec=pltpu.PrefetchScalarGridSpec(
            num_scalar_prefetch=1,
            grid=(1,),
            in_specs=[codes, scales, codes, scales],
            out_specs=pl.BlockSpec(out, lambda k, place_ref: (0, 0, 0, 0)),
        ),
        out_shape=jax.ShapeDtypeStruct(out, jnp.float32),
        compiler_params=pltpu.CompilerParams(vmem_limit_bytes=PIECE_LIMIT),
        name="make_pieces",
    )(place[None], up_codes, up_scales.T, down_codes, down_scales.T)


def narrow_kernel(columns_ref, out_ref):
    out_ref[...] = columns_ref[...].astype(out_ref.dtype)


def narrow(columns):
    n = columns.shape[0]
    block = pl.BlockSpec((n // 2,) + columns.shape[1:], lambda k: (k, 0, 0))
    return pl.pallas_call(
        narrow_kernel,
        grid=(2,),
        in_specs=[block],
        out_specs=block,
        out_shape=jax.ShapeDtypeStruct(columns.shape, jnp.bfloat16),
        compiler_params=pltpu.CompilerParams(vmem_limit_bytes=PIECE_LIMIT),
        cost_estimate=pl.CostEstimate(flops=0, bytes_accessed=12000000, transcendentals=0),
        name="narrow",
    )(columns)


def cut_kernel(tokens_ref, grads_ref, out_ref):
    rows = tokens_ref.shape[0]
    out_ref[:rows] = tokens_ref[...].astype(jnp.float32)
    out_ref[rows:] = grads_ref[...].astype(jnp.float32)


def cut_columns(tokens, grads, n):
    rows, depth = tokens.shape
    cut = pl.BlockSpec((rows, depth // n), lambda k: (0, k))
    return pl.pallas_call(
        cut_kernel,
        grid=(n,),
        in_specs=[cut, cut],
        out_specs=pl.BlockSpec((None, 2 * rows, depth // n), lambda k: (k, 0, 0)),
        out_shape=jax.ShapeDtypeStruct((n, 2 * rows, depth // n), jnp.float32),
        compiler_params=pltpu.CompilerParams(vmem_limit_bytes=VMEM_LIMIT),
        cost_estimate=pl.CostEstimate(flops=0, bytes_accessed=8000000, transcendentals=0),
        name="cut_columns",
    )(tokens, grads)


def node_kernel(core_ref, left_hbm, right_ref, mine_ref, other_ref, left, sems):
    n, kinds, rows, _ = right_ref.shape
    owned = mine_ref.shape[1] // kinds
    arrivals = [pltpu.make_async_copy(left_hbm.at[p], left.at[p], sems.at[p]) for p in range(n)]
    for copy in arrivals:
        copy.start()
    totals = [None] * kinds
    for p in range(n):
        arrivals[p].wait()
        for kind in range(kinds):
            term = lax.dot_general(
                right_ref[p, kind].astype(jnp.bfloat16),
                left[p, kind * rows : (kind + 1) * rows],
                (((0,), (0,)), ((), ())),
                preferred_element_type=jnp.float32,
            )
            clipped = clip_blocks(term)
            totals[kind] = clipped if totals[kind] is None else totals[kind] + clipped
    for kind in range(kinds):
        summed = clip_blocks(totals[kind]).T.reshape(mine_ref.shape[0], 2, owned, mine_ref.shape[2])
        first = core_ref[0] == 0
        part = slice(kind * owned, (kind + 1) * owned)
        mine_ref[:, part] = jnp.where(first, summed[:, 0], summed[:, 1])
        other_ref[:, part] = jnp.where(first, summed[:, 1], summed[:, 0])


def node_sums(core, left, right, owned):
    height = left.shape[2]
    n, kinds, rows, width = right.shape
    half = (height // (2 * owned), kinds * owned, width)
    vmem = pl.BlockSpec(memory_space=pltpu.VMEM)
    return pl.pallas_call(
        node_kernel,
        in_specs=[
            pl.BlockSpec(memory_space=pltpu.SMEM),
            pl.BlockSpec(memory_space=pltpu.HBM),
            vmem,
        ],
        out_specs=[vmem, vmem],
        out_shape=[jax.ShapeDtypeStruct(half, jnp.float32)] * 2,
        scratch_shapes=[pltpu.VMEM(left.shape, left.dtype), pltpu.SemaphoreType.DMA((n,))],
        compiler_params=pltpu.CompilerParams(vmem_limit_bytes=VMEM_LIMIT),
        cost_estimate=pl.CostEstimate(
            flops=4 * n * rows * height * width, bytes_accessed=9000000, transcendentals=0
        ),
        name="node_sums",
    )(core, pltpu.with_memory_space_constraint(left, pltpu.HBM), right)


def local(tokens, out_grad, up_codes, up_scales, down_codes, down_scales):
    n_local = lax.axis_size(LOCAL)
    n_group = lax.axis_size(GROUP)
    devices_all = lax.axis_size(AXES)
    depth = tokens.shape[1]
    owned = depth // devices_all
    core = lax.axis_index("c")

    place = lax.axis_index(GROUP)
    pieces = exchange(
        make_pieces(place, n_group, n_local, up_codes, up_scales, down_codes, down_scales), LOCAL
    )
    pieces, cut = lax.optimization_barrier((pieces, cut_columns(tokens, out_grad, n_local)))
    weights = lax.all_gather(pieces, GROUP, axis=0)
    columns = exchange(cut, LOCAL)
    both = hidden_pass(weights, tokens, out_grad)
    both_all = exchange(both, LOCAL)

    mine, other = node_sums(core[None], narrow(columns), both_all, owned)
    input_grad = input_pass(both, weights)
    pairs = mine + lax.ppermute(other, "c", [(0, 1), (1, 0)])
    owned_sums = exchange(pairs, ("yh", "z"))
    grads = jnp.sum(owned_sums, axis=0) / devices_all
    return (input_grad, grads[:owned], grads[owned:])


def solution(mesh):
    fine = Mesh(mesh.devices.reshape(4, 8, 2, 4, 2), AXES)
    by_tokens = P(AXES, None)
    by_rows = P(LOCAL, None)
    owned_rows = P(LOCAL + ("yh", "z", "c"), None)
    return jax.shard_map(
        local,
        mesh=fine,
        in_specs=(by_tokens, by_tokens, by_rows, by_rows, by_rows, by_rows),
        out_specs=(by_tokens, owned_rows, owned_rows),
        check_vma=False,
    )
```

```python
import functools
import math
import jax
import jax.numpy as jnp
from jax import lax
from jax.experimental import pallas as pl
from jax.experimental.pallas import tpu as pltpu
from jax.sharding import Mesh, PartitionSpec as P

QBLOCK = 128
AXES = ("yh", "z", "c", "x", "yl")
LOCAL = ("x", "yl")
GROUP = ("z", "c")
SHARDS = 2
VMEM_LIMIT = 16 * 1024 * 1024
PASS_LIMIT = 24 * 1024 * 1024
PIECE_LIMIT = 60 * 1024 * 1024


def exchange(array, axes):
    return lax.all_to_all(array, axes, split_axis=0, concat_axis=0, tiled=True)


def clip_blocks(values):
    parts = []
    for k in range(values.shape[0] // QBLOCK):
        block = values[k * QBLOCK : (k + 1) * QBLOCK]
        mean = jnp.mean(block * block, axis=0, keepdims=True) + 1e-06
        root = lax.rsqrt(mean)
        codes = jnp.clip(block * (3.5 * root), -7.0, 7.0).astype(jnp.bfloat16)
        parts.append(codes.astype(jnp.float32) * (mean * root * (2.0 / 7.0)))
    return jnp.concatenate(parts, axis=0)


def inner_tanh(v):
    return jnp.tanh(math.sqrt(2.0 / math.pi) * (v + 0.044715 * v * v * v))


def product(kind, weights_hbm, weights, left, sems):
    n, groups, piece, width = weights.shape
    shard = groups * piece
    copies = [
        pltpu.make_async_copy(weights_hbm.at[:, k, kind], weights.at[k], sems.at[k]) for k in range(n)
    ]
    for copy in copies:
        copy.start()
    total = None
    for k in range(n):
        copies[k].wait()
        block = weights[k].reshape(shard, width).astype(jnp.bfloat16)
        columns = left[:, k * shard : (k + 1) * shard]
        term = jnp.dot(columns, block, preferred_element_type=jnp.float32)
        total = term if total is None else total + term
    return total


def send_all(values, rounded, out_hbm, sems):
    rounded[...] = values.astype(jnp.bfloat16).astype(jnp.float32)
    copies = [
        pltpu.make_async_copy(rounded, out_hbm.at[k], sems.at[k]) for k in range(out_hbm.shape[0])
    ]
    for copy in copies:
        copy.start()
    return copies


def forward_kernel(weights_hbm, tokens_ref, act_hbm, preact_ref, weights, rounded, in_sems, out_sems):
    v = product(0, weights_hbm, weights, tokens_ref, in_sems)
    copies = send_all(0.5 * v * (1.0 + inner_tanh(v)), rounded, act_hbm, out_sems)
    preact_ref[...] = v
    for copy in copies:
        copy.wait()


def backward_kernel(weights_hbm, grads_ref, preact_ref, hidden_hbm, weights, rounded, in_sems, out_sems):
    v = preact_ref[...]
    t = inner_tanh(v)
    slope = 0.5 * (1.0 + t) + 0.5 * v * (1.0 - t * t) * math.sqrt(2.0 / math.pi) * (
        1.0 + 3.0 * 0.044715 * v * v
    )
    back = product(1, weights_hbm, weights, grads_ref, in_sems)
    for copy in send_all(back * slope, rounded, hidden_hbm, out_sems):
        copy.wait()


def pass_params(weights, rows, depth):
    groups, n, _, piece, width = weights.shape
    return dict(
        scratch_shapes=[
            pltpu.VMEM((n, groups, piece, width), jnp.float32),
            pltpu.VMEM((rows, width), jnp.float32),
            pltpu.SemaphoreType.DMA((n,)),
            pltpu.SemaphoreType.DMA((n,)),
        ],
        compiler_params=pltpu.CompilerParams(vmem_limit_bytes=PASS_LIMIT),
        cost_estimate=pl.CostEstimate(
            flops=2 * rows * depth * width, bytes_accessed=8000000, transcendentals=rows * width
        ),
    )


def forward(weights, tokens):
    _, n, _, _, width = weights.shape
    rows, depth = tokens.shape
    hbm, vmem = pl.BlockSpec(memory_space=pltpu.HBM), pl.BlockSpec(memory_space=pltpu.VMEM)
    return pl.pallas_call(
        forward_kernel,
        in_specs=[hbm, vmem],
        out_specs=[hbm, vmem],
        out_shape=[
            pltpu.HBM((n, rows, width), jnp.float32),
            jax.ShapeDtypeStruct((rows, width), jnp.float32),
        ],
        name="forward",
        **pass_params(weights, rows, depth),
    )(pltpu.with_memory_space_constraint(weights, pltpu.HBM), tokens)


def backward(weights, grads, preact):
    _, n, _, _, width = weights.shape
    rows, depth = grads.shape
    hbm, vmem = pl.BlockSpec(memory_space=pltpu.HBM), pl.BlockSpec(memory_space=pltpu.VMEM)
    return pl.pallas_call(
        backward_kernel,
        in_specs=[hbm, vmem, vmem],
        out_specs=hbm,
        out_shape=pltpu.HBM((n, rows, width), jnp.float32),
        name="backward",
        **pass_params(weights, rows, depth),
    )(pltpu.with_memory_space_constraint(weights, pltpu.HBM), grads, preact)


def input_kernel(hidden_ref, weights_ref, out_ref):
    _, shards, _, width = weights_ref.shape
    shard = out_ref.shape[1] // shards
    hidden = hidden_ref[...].astype(jnp.bfloat16)
    for q in range(shards):
        up = weights_ref[:, q].reshape(shard, width).astype(jnp.bfloat16)
        out_ref[:, q * shard : (q + 1) * shard] = lax.dot_general(
            hidden, up, (((1,), (1,)), ((), ())), preferred_element_type=jnp.float32
        ).astype(out_ref.dtype)


def input_pass(hidden, weights):
    groups, n, _, piece, width = weights.shape
    rows = hidden.shape[1]
    depth = groups * n * piece
    return pl.pallas_call(
        input_kernel,
        grid=(n // SHARDS,),
        in_specs=[
            pl.BlockSpec((None, rows, width), lambda k: (0, 0, 0)),
            pl.BlockSpec((groups, SHARDS, None, piece, width), lambda k: (0, k, 0, 0, 0)),
        ],
        out_specs=pl.BlockSpec((rows, SHARDS * depth // n), lambda k: (0, k)),
        out_shape=jax.ShapeDtypeStruct((rows, depth), jnp.bfloat16),
        compiler_params=pltpu.CompilerParams(vmem_limit_bytes=VMEM_LIMIT),
        cost_estimate=pl.CostEstimate(
            flops=2 * rows * depth * width, bytes_accessed=6000000, transcendentals=0
        ),
        name="input_pass",
    )(hidden, weights)


def piece_kernel(place_ref, up_ref, up_scales_ref, down_ref, down_scales_ref, out_ref):
    piece, width = up_ref.shape
    shard = up_scales_ref.shape[1]
    shape = (piece, shard)
    wanted = lax.broadcasted_iota(jnp.int32, shape, 0) + place_ref[0] * piece
    chosen = wanted == lax.broadcasted_iota(jnp.int32, shape, 1)
    for kind, (codes, scales) in enumerate(((up_ref, up_scales_ref), (down_ref, down_scales_ref))):
        for k in range(width // QBLOCK):
            own = jnp.sum(jnp.where(chosen, scales[k : k + 1], 0.0), axis=1, keepdims=True)
            columns = slice(k * QBLOCK, (k + 1) * QBLOCK)
            product = codes[:, columns].astype(jnp.float32) * own
            for p in range(out_ref.shape[0]):
                out_ref[p, kind, :, columns] = product


def make_pieces(place, n_group, n_local, up_codes, up_scales, down_codes, down_scales):
    shard, width = up_codes.shape
    piece = shard // n_group
    codes = pl.BlockSpec((piece, width), lambda k, place_ref: (place_ref[0], 0))
    scales = pl.BlockSpec(up_scales.T.shape, lambda k, place_ref: (0, 0))
    out = (n_local, 2, piece, width)
    return pl.pallas_call(
        piece_kernel,
        grid_spec=pltpu.PrefetchScalarGridSpec(
            num_scalar_prefetch=1,
            grid=(1,),
            in_specs=[codes, scales, codes, scales],
            out_specs=pl.BlockSpec(out, lambda k, place_ref: (0, 0, 0, 0)),
        ),
        out_shape=jax.ShapeDtypeStruct(out, jnp.float32),
        compiler_params=pltpu.CompilerParams(vmem_limit_bytes=PIECE_LIMIT),
        name="make_pieces",
    )(place[None], up_codes, up_scales.T, down_codes, down_scales.T)


def narrow_kernel(columns_ref, out_ref):
    out_ref[...] = columns_ref[...].astype(out_ref.dtype)


def narrow(columns):
    n = columns.shape[0]
    block = pl.BlockSpec((n // 2,) + columns.shape[1:], lambda k: (k, 0, 0))
    return pl.pallas_call(
        narrow_kernel,
        grid=(2,),
        in_specs=[block],
        out_specs=block,
        out_shape=jax.ShapeDtypeStruct(columns.shape, jnp.bfloat16),
        compiler_params=pltpu.CompilerParams(vmem_limit_bytes=PIECE_LIMIT),
        cost_estimate=pl.CostEstimate(flops=0, bytes_accessed=12000000, transcendentals=0),
        name="narrow",
    )(columns)


def cut_kernel(tokens_ref, grads_ref, out_ref):
    rows = tokens_ref.shape[0]
    out_ref[:rows] = tokens_ref[...].astype(jnp.float32)
    out_ref[rows:] = grads_ref[...].astype(jnp.float32)


def cut_columns(tokens, grads, n):
    rows, depth = tokens.shape
    cut = pl.BlockSpec((rows, depth // n), lambda k: (0, k))
    return pl.pallas_call(
        cut_kernel,
        grid=(n,),
        in_specs=[cut, cut],
        out_specs=pl.BlockSpec((None, 2 * rows, depth // n), lambda k: (k, 0, 0)),
        out_shape=jax.ShapeDtypeStruct((n, 2 * rows, depth // n), jnp.float32),
        compiler_params=pltpu.CompilerParams(vmem_limit_bytes=VMEM_LIMIT),
        cost_estimate=pl.CostEstimate(flops=0, bytes_accessed=8000000, transcendentals=0),
        name="cut_columns",
    )(tokens, grads)


def node_kernel(kind, core_ref, left_hbm, right_ref, mine_ref, other_ref, left, sems):
    n, rows, width = right_ref.shape
    copies = [
        pltpu.make_async_copy(
            left_hbm.at[p, pl.ds(kind * rows, rows)], left.at[p], sems.at[p]
        )
        for p in range(n)
    ]
    for copy in copies:
        copy.start()
    total = None
    for p in range(n):
        copies[p].wait()
        term = lax.dot_general(
            right_ref[p].astype(jnp.bfloat16),
            left[p],
            (((0,), (0,)), ((), ())),
            preferred_element_type=jnp.float32,
        )
        clipped = clip_blocks(term)
        total = clipped if total is None else total + clipped
    pairs, owned, _ = mine_ref.shape
    summed = clip_blocks(total).T.reshape(pairs, 2, owned, width)
    first = core_ref[0] == 0
    mine_ref[...] = jnp.where(first, summed[:, 0], summed[:, 1])
    other_ref[...] = jnp.where(first, summed[:, 1], summed[:, 0])


def node_sum(core, left, kind, right, owned):
    height = left.shape[2]
    n, rows, width = right.shape
    half = (height // (2 * owned), owned, width)
    vmem = pl.BlockSpec(memory_space=pltpu.VMEM)
    return pl.pallas_call(
        functools.partial(node_kernel, kind),
        in_specs=[
            pl.BlockSpec(memory_space=pltpu.SMEM),
            pl.BlockSpec(memory_space=pltpu.HBM),
            vmem,
        ],
        out_specs=[vmem, vmem],
        out_shape=[jax.ShapeDtypeStruct(half, jnp.float32)] * 2,
        scratch_shapes=[pltpu.VMEM((n, rows, height), left.dtype), pltpu.SemaphoreType.DMA((n,))],
        compiler_params=pltpu.CompilerParams(vmem_limit_bytes=VMEM_LIMIT),
        cost_estimate=pl.CostEstimate(
            flops=2 * n * rows * height * width, bytes_accessed=5000000, transcendentals=0
        ),
        name="node_sum",
    )(core, pltpu.with_memory_space_constraint(left, pltpu.HBM), right)


def local(tokens, out_grad, up_codes, up_scales, down_codes, down_scales):
    n_local = lax.axis_size(LOCAL)
    n_group = lax.axis_size(GROUP)
    devices_all = lax.axis_size(AXES)
    depth = tokens.shape[1]
    owned = depth // devices_all
    core = lax.axis_index("c")

    place = lax.axis_index(GROUP)
    pieces = exchange(
        make_pieces(place, n_group, n_local, up_codes, up_scales, down_codes, down_scales), LOCAL
    )
    pieces, cut = lax.optimization_barrier((pieces, cut_columns(tokens, out_grad, n_local)))
    weights = lax.all_gather(pieces, GROUP, axis=0)
    columns = exchange(cut, LOCAL)
    activated, preact = forward(weights, tokens)
    activated_all = exchange(activated, LOCAL)
    hidden = backward(weights, out_grad, preact)
    hidden_all = exchange(hidden, LOCAL)
    narrowed = narrow(columns)

    def over_cores(kind, right):
        mine, other = node_sum(core[None], narrowed, kind, right, owned)
        return mine + lax.ppermute(other, "c", [(0, 1), (1, 0)])

    grad_down = over_cores(1, activated_all)
    grad_up = over_cores(0, hidden_all)
    input_grad = input_pass(hidden, weights)
    owned_sums = exchange(jnp.concatenate([grad_up, grad_down], axis=1), ("yh", "z"))
    grads = jnp.sum(owned_sums, axis=0) / devices_all
    return (input_grad, grads[:owned], grads[owned:])


def solution(mesh):
    fine = Mesh(mesh.devices.reshape(4, 8, 2, 4, 2), AXES)
    by_tokens = P(AXES, None)
    by_rows = P(LOCAL, None)
    owned_rows = P(LOCAL + ("yh", "z", "c"), None)
    return jax.shard_map(
        local,
        mesh=fine,
        in_specs=(by_tokens, by_tokens, by_rows, by_rows, by_rows, by_rows),
        out_specs=(by_tokens, owned_rows, owned_rows),
        check_vma=False,
    )
```

```python
import functools
import math
import jax
import jax.numpy as jnp
from jax import lax
from jax.experimental import pallas as pl
from jax.experimental.pallas import tpu as pltpu
from jax.sharding import Mesh, PartitionSpec as P

QBLOCK = 128
SWAP = ((0, 1), (1, 0))
AXES = ("yh", "z", "c", "x", "yl")
LOCAL = ("x", "yl")
GROUP = ("z", "c")
SHARDS = 2
VMEM_LIMIT = 16 * 1024 * 1024
HIDDEN_LIMIT = 52 * 1024 * 1024
PIECE_LIMIT = 60 * 1024 * 1024


def exchange(array, axes):
    return lax.all_to_all(array, axes, split_axis=0, concat_axis=0, tiled=True)


def clip_blocks(values):
    parts = []
    for k in range(values.shape[0] // QBLOCK):
        block = values[k * QBLOCK : (k + 1) * QBLOCK]
        mean = jnp.mean(block * block, axis=0, keepdims=True) + 1e-06
        largest = 2.0 * (mean * lax.rsqrt(mean))
        parts.append(jnp.minimum(jnp.maximum(block, -largest), largest))
    return jnp.concatenate(parts, axis=0)


def inner_tanh(v):
    return jnp.tanh(math.sqrt(2.0 / math.pi) * (v + 0.044715 * v * v * v))


def hidden_kernel(
    weights_hbm, tokens_ref, grads_ref, act_hbm, hidden_ref, weights, act, pre, back, in_sems, out_sems
):
    n, groups, _, piece, width = weights.shape
    shard = groups * piece
    arrivals = [
        pltpu.make_async_copy(weights_hbm.at[:, k], weights.at[k], in_sems.at[k]) for k in range(n)
    ]
    for copy in arrivals:
        copy.start()
    pre[...] = jnp.zeros_like(pre)
    back[...] = jnp.zeros_like(back)
    for k in range(n):
        arrivals[k].wait()
        up = weights[k, :, 0].reshape(shard, width).astype(jnp.bfloat16)
        down = weights[k, :, 1].reshape(shard, width).astype(jnp.bfloat16)
        columns = slice(k * shard, (k + 1) * shard)
        pre[...] += jnp.dot(tokens_ref[:, columns], up, preferred_element_type=jnp.float32)
        back[...] += jnp.dot(grads_ref[:, columns], down, preferred_element_type=jnp.float32)
    v = pre[...]
    t = inner_tanh(v)
    act[...] = (0.5 * v * (1.0 + t)).astype(jnp.bfloat16).astype(jnp.float32)
    copies = act_hbm.shape[0]
    departures = [pltpu.make_async_copy(act, act_hbm.at[k], out_sems.at[k]) for k in range(copies)]
    for copy in departures:
        copy.start()
    slope = 0.5 * (1.0 + t) + 0.5 * v * (1.0 - t * t) * math.sqrt(2.0 / math.pi) * (
        1.0 + 3.0 * 0.044715 * v * v
    )
    hidden_ref[...] = (back[...] * slope).astype(jnp.bfloat16).astype(jnp.float32)
    for copy in departures:
        copy.wait()


def hidden_pass(weights, tokens, grads, copies):
    groups, n, kinds, piece, width = weights.shape
    rows, depth = tokens.shape
    return pl.pallas_call(
        hidden_kernel,
        in_specs=[
            pl.BlockSpec(memory_space=pltpu.HBM),
            pl.BlockSpec(memory_space=pltpu.VMEM),
            pl.BlockSpec(memory_space=pltpu.VMEM),
        ],
        out_specs=[pl.BlockSpec(memory_space=pltpu.HBM), pl.BlockSpec(memory_space=pltpu.VMEM)],
        out_shape=[
            pltpu.HBM((copies, rows, width), jnp.float32),
            jax.ShapeDtypeStruct((rows, width), jnp.float32),
        ],
        scratch_shapes=[
            pltpu.VMEM((n, groups, kinds, piece, width), jnp.float32),
            pltpu.VMEM((rows, width), jnp.float32),
            pltpu.VMEM((rows, width), jnp.float32),
            pltpu.VMEM((rows, width), jnp.float32),
            pltpu.SemaphoreType.DMA((n,)),
            pltpu.SemaphoreType.DMA((copies,)),
        ],
        compiler_params=pltpu.CompilerParams(vmem_limit_bytes=HIDDEN_LIMIT),
        cost_estimate=pl.CostEstimate(
            flops=4 * rows * depth * width, bytes_accessed=13000000, transcendentals=rows * width
        ),
        name="hidden_pass",
    )(weights, tokens, grads)


def input_kernel(hidden_ref, weights_ref, out_ref):
    _, shards, _, width = weights_ref.shape
    shard = out_ref.shape[1] // shards
    hidden = hidden_ref[...].astype(jnp.bfloat16)
    for q in range(shards):
        up = weights_ref[:, q].reshape(shard, width).astype(jnp.bfloat16)
        out_ref[:, q * shard : (q + 1) * shard] = lax.dot_general(
            hidden, up, (((1,), (1,)), ((), ())), preferred_element_type=jnp.float32
        ).astype(out_ref.dtype)


def input_pass(hidden, weights):
    groups, n, _, piece, width = weights.shape
    rows = hidden.shape[0]
    depth = groups * n * piece
    return pl.pallas_call(
        input_kernel,
        grid=(n // SHARDS,),
        in_specs=[
            pl.BlockSpec((rows, width), lambda k: (0, 0)),
            pl.BlockSpec((groups, SHARDS, None, piece, width), lambda k: (0, k, 0, 0, 0)),
        ],
        out_specs=pl.BlockSpec((rows, SHARDS * depth // n), lambda k: (0, k)),
        out_shape=jax.ShapeDtypeStruct((rows, depth), jnp.bfloat16),
        compiler_params=pltpu.CompilerParams(vmem_limit_bytes=VMEM_LIMIT),
        cost_estimate=pl.CostEstimate(
            flops=2 * rows * depth * width, bytes_accessed=6000000, transcendentals=0
        ),
        name="input_pass",
    )(hidden, weights)


def piece_kernel(place_ref, up_ref, up_scales_ref, down_ref, down_scales_ref, out_ref):
    piece, width = up_ref.shape
    shard = up_scales_ref.shape[1]
    shape = (piece, shard)
    wanted = lax.broadcasted_iota(jnp.int32, shape, 0) + place_ref[0] * piece
    chosen = wanted == lax.broadcasted_iota(jnp.int32, shape, 1)
    for kind, (codes, scales) in enumerate(((up_ref, up_scales_ref), (down_ref, down_scales_ref))):
        for k in range(width // QBLOCK):
            own = jnp.sum(jnp.where(chosen, scales[k : k + 1], 0.0), axis=1, keepdims=True)
            columns = slice(k * QBLOCK, (k + 1) * QBLOCK)
            product = codes[:, columns].astype(jnp.float32) * own
            for p in range(out_ref.shape[0]):
                out_ref[p, kind, :, columns] = product


def make_pieces(place, n_group, n_local, up_codes, up_scales, down_codes, down_scales):
    shard, width = up_codes.shape
    piece = shard // n_group
    codes = pl.BlockSpec((piece, width), lambda k, place_ref: (place_ref[0], 0))
    scales = pl.BlockSpec(up_scales.T.shape, lambda k, place_ref: (0, 0))
    out = (n_local, 2, piece, width)
    return pl.pallas_call(
        piece_kernel,
        grid_spec=pltpu.PrefetchScalarGridSpec(
            num_scalar_prefetch=1,
            grid=(1,),
            in_specs=[codes, scales, codes, scales],
            out_specs=pl.BlockSpec(out, lambda k, place_ref: (0, 0, 0, 0)),
        ),
        out_shape=jax.ShapeDtypeStruct(out, jnp.float32),
        compiler_params=pltpu.CompilerParams(vmem_limit_bytes=PIECE_LIMIT),
        name="make_pieces",
    )(place[None], up_codes, up_scales.T, down_codes, down_scales.T)


def narrow_kernel(columns_ref, out_ref):
    out_ref[...] = columns_ref[...].astype(out_ref.dtype)


def narrow(columns):
    n = columns.shape[0]
    block = pl.BlockSpec((n // 2,) + columns.shape[1:], lambda k: (k, 0, 0))
    return pl.pallas_call(
        narrow_kernel,
        grid=(2,),
        in_specs=[block],
        out_specs=block,
        out_shape=jax.ShapeDtypeStruct(columns.shape, jnp.bfloat16),
        compiler_params=pltpu.CompilerParams(vmem_limit_bytes=PIECE_LIMIT),
        cost_estimate=pl.CostEstimate(flops=0, bytes_accessed=12000000, transcendentals=0),
        name="narrow",
    )(columns)


def cut_kernel(tokens_ref, grads_ref, out_ref):
    rows = tokens_ref.shape[0]
    out_ref[:rows] = tokens_ref[...].astype(jnp.float32)
    out_ref[rows:] = grads_ref[...].astype(jnp.float32)


def cut_columns(tokens, grads, n):
    rows, depth = tokens.shape
    cut = pl.BlockSpec((rows, depth // n), lambda k: (0, k))
    return pl.pallas_call(
        cut_kernel,
        grid=(n,),
        in_specs=[cut, cut],
        out_specs=pl.BlockSpec((None, 2 * rows, depth // n), lambda k: (k, 0, 0)),
        out_shape=jax.ShapeDtypeStruct((n, 2 * rows, depth // n), jnp.float32),
        compiler_params=pltpu.CompilerParams(vmem_limit_bytes=VMEM_LIMIT),
        cost_estimate=pl.CostEstimate(flops=0, bytes_accessed=8000000, transcendentals=0),
        name="cut_columns",
    )(tokens, grads)


def node_kernel(place_ref, left_hbm, hidden_ref, act_ref, act_peer_ref, mine_ref, other_ref, left, sems):
    rows, width = act_ref.shape[1:]
    n = left.shape[0]
    copies = [
        pltpu.make_async_copy(
            left_hbm.at[2 * (p // 2) + lax.rem(place_ref[1] + p, 2)], left.at[p], sems.at[p]
        )
        for p in range(n)
    ]
    for copy in copies:
        copy.start()
    totals = [None, None]
    for p in range(n):
        copies[p].wait()
        rights = (hidden_ref[p // 2, p % 2], (act_peer_ref if p % 2 else act_ref)[p // 2])
        for kind in range(2):
            term = lax.dot_general(
                rights[kind].astype(jnp.bfloat16),
                left[p, kind * rows : (kind + 1) * rows],
                (((0,), (0,)), ((), ())),
                preferred_element_type=jnp.float32,
            )
            clipped = clip_blocks(term)
            totals[kind] = clipped if totals[kind] is None else totals[kind] + clipped
    owned = mine_ref.shape[1] // 2
    for kind in range(2):
        summed = clip_blocks(totals[kind]).T.reshape(mine_ref.shape[0], 2, owned, width)
        first = place_ref[0] == 0
        part = slice(kind * owned, (kind + 1) * owned)
        mine_ref[:, part] = jnp.where(first, summed[:, 0], summed[:, 1])
        other_ref[:, part] = jnp.where(first, summed[:, 1], summed[:, 0])


def node_sums(place, left, hidden, act, act_peer, owned):
    n, _, height = left.shape
    _, rows, width = act.shape
    half = (height // (2 * owned), 2 * owned, width)
    vmem = pl.BlockSpec(memory_space=pltpu.VMEM)
    return pl.pallas_call(
        node_kernel,
        in_specs=[
            pl.BlockSpec(memory_space=pltpu.SMEM),
            pl.BlockSpec(memory_space=pltpu.HBM),
            vmem,
            vmem,
            vmem,
        ],
        out_specs=[vmem, vmem],
        out_shape=[jax.ShapeDtypeStruct(half, jnp.float32)] * 2,
        scratch_shapes=[pltpu.VMEM(left.shape, left.dtype), pltpu.SemaphoreType.DMA((n,))],
        compiler_params=pltpu.CompilerParams(vmem_limit_bytes=VMEM_LIMIT),
        cost_estimate=pl.CostEstimate(
            flops=4 * n * rows * height * width, bytes_accessed=9000000, transcendentals=0
        ),
        name="node_sums",
    )(place, pltpu.with_memory_space_constraint(left, pltpu.HBM), hidden, act, act_peer)


def local(tokens, out_grad, up_codes, up_scales, down_codes, down_scales):
    n_local = lax.axis_size(LOCAL)
    n_group = lax.axis_size(GROUP)
    devices_all = lax.axis_size(AXES)
    depth = tokens.shape[1]
    owned = depth // devices_all
    core = lax.axis_index("c")

    place = lax.axis_index(GROUP)
    pieces = exchange(
        make_pieces(place, n_group, n_local, up_codes, up_scales, down_codes, down_scales), LOCAL
    )
    pieces, cut = lax.optimization_barrier((pieces, cut_columns(tokens, out_grad, n_local)))
    weights = lax.all_gather(pieces, GROUP, axis=0)
    columns = exchange(cut, LOCAL)
    n_x = lax.axis_size("x")
    act_copies, hidden = hidden_pass(weights, tokens, out_grad, n_x)
    hidden_peer = lax.ppermute(hidden, "yl", SWAP)
    columns, act_copies = lax.optimization_barrier((columns, act_copies))
    act_all = exchange(act_copies, "x")
    hidden_pair = jnp.stack([hidden, hidden_peer])
    hidden_copies = jnp.broadcast_to(hidden_pair[None], (n_x,) + hidden_pair.shape)
    act_all, hidden_copies = lax.optimization_barrier((act_all, hidden_copies))
    act_peer_all = lax.ppermute(act_all, "yl", SWAP)
    hidden_all = exchange(hidden_copies, "x")
    place = jnp.stack([core, lax.axis_index("yl")])
    mine, other = node_sums(place, narrow(columns), hidden_all, act_all, act_peer_all, owned)
    input_grad = input_pass(hidden, weights)
    pairs = mine + lax.ppermute(other, "c", SWAP)
    owned_sums = exchange(pairs, ("yh", "z"))
    grads = jnp.sum(owned_sums, axis=0) / devices_all
    return (input_grad, grads[:owned], grads[owned:])


def solution(mesh):
    fine = Mesh(mesh.devices.reshape(4, 8, 2, 4, 2), AXES)
    by_tokens = P(AXES, None)
    by_rows = P(LOCAL, None)
    owned_rows = P(LOCAL + ("yh", "z", "c"), None)
    return jax.shard_map(
        local,
        mesh=fine,
        in_specs=(by_tokens, by_tokens, by_rows, by_rows, by_rows, by_rows),
        out_specs=(by_tokens, owned_rows, owned_rows),
        check_vma=False,
    )
```

```python
import functools
import math
import jax
import jax.numpy as jnp
from jax import lax
from jax.experimental import pallas as pl
from jax.experimental.pallas import tpu as pltpu
from jax.sharding import Mesh, PartitionSpec as P

QBLOCK = 128
SWAP = ((0, 1), (1, 0))
AXES = ("yh", "z", "c", "x", "yl")
LOCAL = ("x", "yl")
GROUP = ("z", "c")
SHARDS = 2
VMEM_LIMIT = 16 * 1024 * 1024
HIDDEN_LIMIT = 20 * 1024 * 1024


def in_hbm(array):
    return pltpu.with_memory_space_constraint(array, pltpu.HBM)


def exchange(array, axes):
    return lax.all_to_all(array, axes, split_axis=0, concat_axis=0, tiled=True)


def clip_blocks(values):
    parts = []
    for k in range(values.shape[0] // QBLOCK):
        block = values[k * QBLOCK : (k + 1) * QBLOCK]
        mean = jnp.mean(block * block, axis=0, keepdims=True) + 1e-06
        largest = 2.0 * (mean * lax.rsqrt(mean))
        parts.append(jnp.minimum(jnp.maximum(block, -largest), largest))
    return jnp.concatenate(parts, axis=0)


def inner_tanh(v):
    return jnp.tanh(math.sqrt(2.0 / math.pi) * (v + 0.044715 * v * v * v))


def hidden_kernel(
    weights_hbm, tokens_ref, grads_ref, act_hbm, hidden_ref, weights, act, in_sems, out_sems
):
    kinds, n, groups, piece, width = weights.shape
    shard = groups * piece
    arrivals = [
        [
            pltpu.make_async_copy(weights_hbm.at[:, k, kind], weights.at[kind, k], in_sems.at[kind, k])
            for k in range(n)
        ]
        for kind in range(kinds)
    ]
    for copy in arrivals[0] + arrivals[1]:
        copy.start()

    def product(kind, left):
        total = None
        for k in range(n):
            arrivals[kind][k].wait()
            block = weights[kind, k].reshape(shard, width).astype(jnp.bfloat16)
            columns = left[:, k * shard : (k + 1) * shard]
            term = jnp.dot(columns, block, preferred_element_type=jnp.float32)
            total = term if total is None else total + term
        return total

    v = product(0, tokens_ref)
    t = inner_tanh(v)
    act[...] = (0.5 * v * (1.0 + t)).astype(jnp.bfloat16).astype(jnp.float32)
    copies = act_hbm.shape[0]
    departures = [pltpu.make_async_copy(act, act_hbm.at[k], out_sems.at[k]) for k in range(copies)]
    for copy in departures:
        copy.start()
    slope = 0.5 * (1.0 + t) + 0.5 * v * (1.0 - t * t) * math.sqrt(2.0 / math.pi) * (
        1.0 + 3.0 * 0.044715 * v * v
    )
    back = product(1, grads_ref)
    hidden_ref[...] = (back * slope).astype(jnp.bfloat16).astype(jnp.float32)
    for copy in departures:
        copy.wait()


def hidden_pass(weights, tokens, grads, copies):
    groups, n, kinds, piece, width = weights.shape
    rows, depth = tokens.shape
    return pl.pallas_call(
        hidden_kernel,
        in_specs=[
            pl.BlockSpec(memory_space=pltpu.HBM),
            pl.BlockSpec(memory_space=pltpu.VMEM),
            pl.BlockSpec(memory_space=pltpu.VMEM),
        ],
        out_specs=[pl.BlockSpec(memory_space=pltpu.HBM), pl.BlockSpec(memory_space=pltpu.VMEM)],
        out_shape=[
            pltpu.HBM((copies, rows, width), jnp.float32),
            jax.ShapeDtypeStruct((rows, width), jnp.float32),
        ],
        scratch_shapes=[
            pltpu.VMEM((kinds, n, groups, piece, width), jnp.float32),
            pltpu.VMEM((rows, width), jnp.float32),
            pltpu.SemaphoreType.DMA((kinds, n)),
            pltpu.SemaphoreType.DMA((copies,)),
        ],
        compiler_params=pltpu.CompilerParams(vmem_limit_bytes=HIDDEN_LIMIT),
        cost_estimate=pl.CostEstimate(
            flops=4 * rows * depth * width, bytes_accessed=13000000, transcendentals=rows * width
        ),
        name="hidden_pass",
    )(in_hbm(weights), tokens, grads)


def input_kernel(hidden_ref, weights_ref, out_ref):
    _, shards, _, width = weights_ref.shape
    shard = out_ref.shape[1] // shards
    hidden = hidden_ref[...].astype(jnp.bfloat16)
    for q in range(shards):
        up = weights_ref[:, q].reshape(shard, width).astype(jnp.bfloat16)
        out_ref[:, q * shard : (q + 1) * shard] = lax.dot_general(
            hidden, up, (((1,), (1,)), ((), ())), preferred_element_type=jnp.float32
        ).astype(out_ref.dtype)


def input_pass(hidden, weights):
    groups, n, _, piece, width = weights.shape
    rows = hidden.shape[0]
    depth = groups * n * piece
    return pl.pallas_call(
        input_kernel,
        grid=(n // SHARDS,),
        in_specs=[
            pl.BlockSpec((rows, width), lambda k: (0, 0)),
            pl.BlockSpec((groups, SHARDS, None, piece, width), lambda k: (0, k, 0, 0, 0)),
        ],
        out_specs=pl.BlockSpec((rows, SHARDS * depth // n), lambda k: (0, k)),
        out_shape=jax.ShapeDtypeStruct((rows, depth), jnp.bfloat16),
        compiler_params=pltpu.CompilerParams(vmem_limit_bytes=VMEM_LIMIT),
        cost_estimate=pl.CostEstimate(
            flops=2 * rows * depth * width, bytes_accessed=6000000, transcendentals=0
        ),
        name="input_pass",
    )(hidden, weights)


def piece_kernel(place_ref, up_ref, up_scales_ref, down_ref, down_scales_ref, out_ref):
    piece, width = up_ref.shape
    shard = up_scales_ref.shape[1]
    shape = (piece, shard)
    wanted = lax.broadcasted_iota(jnp.int32, shape, 0) + place_ref[0] * piece
    chosen = wanted == lax.broadcasted_iota(jnp.int32, shape, 1)
    for kind, (codes, scales) in enumerate(((up_ref, up_scales_ref), (down_ref, down_scales_ref))):
        for k in range(width // QBLOCK):
            own = jnp.sum(jnp.where(chosen, scales[k : k + 1], 0.0), axis=1, keepdims=True)
            columns = slice(k * QBLOCK, (k + 1) * QBLOCK)
            product = codes[:, columns].astype(jnp.float32) * own
            for p in range(out_ref.shape[0]):
                out_ref[p, kind, :, columns] = product


def make_pieces(place, n_group, n_local, up_codes, up_scales, down_codes, down_scales):
    shard, width = up_codes.shape
    piece = shard // n_group
    codes = pl.BlockSpec((piece, width), lambda k, place_ref: (place_ref[0], 0))
    scales = pl.BlockSpec(up_scales.T.shape, lambda k, place_ref: (0, 0))
    out = (n_local, 2, piece, width)
    return pl.pallas_call(
        piece_kernel,
        grid_spec=pltpu.PrefetchScalarGridSpec(
            num_scalar_prefetch=1,
            grid=(1,),
            in_specs=[codes, scales, codes, scales],
            out_specs=pl.BlockSpec(out, lambda k, place_ref: (0, 0, 0, 0)),
        ),
        out_shape=jax.ShapeDtypeStruct(out, jnp.float32),
        compiler_params=pltpu.CompilerParams(vmem_limit_bytes=VMEM_LIMIT),
        name="make_pieces",
    )(
        place[None],
        in_hbm(up_codes),
        in_hbm(up_scales.T),
        in_hbm(down_codes),
        in_hbm(down_scales.T),
    )


def narrow_kernel(columns_ref, out_ref):
    out_ref[...] = columns_ref[...].astype(out_ref.dtype)


def narrow(columns):
    n = columns.shape[0]
    block = pl.BlockSpec((n // 2,) + columns.shape[1:], lambda k: (k, 0, 0))
    return pl.pallas_call(
        narrow_kernel,
        grid=(2,),
        in_specs=[block],
        out_specs=block,
        out_shape=jax.ShapeDtypeStruct(columns.shape, jnp.bfloat16),
        compiler_params=pltpu.CompilerParams(vmem_limit_bytes=VMEM_LIMIT),
        cost_estimate=pl.CostEstimate(flops=0, bytes_accessed=12000000, transcendentals=0),
        name="narrow",
    )(columns)


def cut_kernel(tokens_ref, grads_ref, out_ref):
    rows = tokens_ref.shape[0]
    out_ref[:rows] = tokens_ref[...].astype(jnp.float32)
    out_ref[rows:] = grads_ref[...].astype(jnp.float32)


def cut_columns(tokens, grads, n):
    rows, depth = tokens.shape
    cut = pl.BlockSpec((rows, depth // n), lambda k: (0, k))
    return pl.pallas_call(
        cut_kernel,
        grid=(n,),
        in_specs=[cut, cut],
        out_specs=pl.BlockSpec((None, 2 * rows, depth // n), lambda k: (k, 0, 0)),
        out_shape=jax.ShapeDtypeStruct((n, 2 * rows, depth // n), jnp.float32),
        compiler_params=pltpu.CompilerParams(vmem_limit_bytes=VMEM_LIMIT),
        cost_estimate=pl.CostEstimate(flops=0, bytes_accessed=8000000, transcendentals=0),
        name="cut_columns",
    )(tokens, grads)


def node_kernel(place_ref, left, hidden_ref, act_ref, act_peer_ref, mine_ref, other_ref):
    rows, width = act_ref.shape[1:]
    n = left.shape[0]
    totals = [None, None]
    for p in range(n):
        owner = 2 * (p // 2) + lax.rem(place_ref[1] + p, 2)
        rights = (hidden_ref[p // 2, p % 2], (act_peer_ref if p % 2 else act_ref)[p // 2])
        for kind in range(2):
            term = lax.dot_general(
                rights[kind].astype(jnp.bfloat16),
                left[owner, kind * rows : (kind + 1) * rows],
                (((0,), (0,)), ((), ())),
                preferred_element_type=jnp.float32,
            )
            clipped = clip_blocks(term)
            totals[kind] = clipped if totals[kind] is None else totals[kind] + clipped
    owned = mine_ref.shape[1] // 2
    for kind in range(2):
        summed = clip_blocks(totals[kind]).T.reshape(mine_ref.shape[0], 2, owned, width)
        first = place_ref[0] == 0
        part = slice(kind * owned, (kind + 1) * owned)
        mine_ref[:, part] = jnp.where(first, summed[:, 0], summed[:, 1])
        other_ref[:, part] = jnp.where(first, summed[:, 1], summed[:, 0])


def node_sums(place, left, hidden, act, act_peer, owned):
    height = left.shape[2]
    n, rows, width = 2 * act.shape[0], act.shape[1], act.shape[2]
    half = (height // (2 * owned), 2 * owned, width)
    vmem = pl.BlockSpec(memory_space=pltpu.VMEM)
    return pl.pallas_call(
        node_kernel,
        in_specs=[
            pl.BlockSpec(memory_space=pltpu.SMEM),
            vmem,
            vmem,
            vmem,
            vmem,
        ],
        out_specs=[vmem, vmem],
        out_shape=[jax.ShapeDtypeStruct(half, jnp.float32)] * 2,
        compiler_params=pltpu.CompilerParams(vmem_limit_bytes=VMEM_LIMIT),
        cost_estimate=pl.CostEstimate(
            flops=4 * n * rows * height * width, bytes_accessed=9000000, transcendentals=0
        ),
        name="node_sums",
    )(place, left, hidden, act, act_peer)


def local(tokens, out_grad, up_codes, up_scales, down_codes, down_scales):
    n_local = lax.axis_size(LOCAL)
    n_group = lax.axis_size(GROUP)
    devices_all = lax.axis_size(AXES)
    depth = tokens.shape[1]
    owned = depth // devices_all
    core = lax.axis_index("c")

    place = lax.axis_index(GROUP)
    pieces = exchange(
        make_pieces(place, n_group, n_local, up_codes, up_scales, down_codes, down_scales), LOCAL
    )
    pieces, cut = lax.optimization_barrier((pieces, cut_columns(tokens, out_grad, n_local)))
    weights = lax.all_gather(pieces, GROUP, axis=0)
    columns = exchange(cut, LOCAL)
    n_x = lax.axis_size("x")
    act_copies, hidden = hidden_pass(weights, tokens, out_grad, n_x)
    hidden_peer = lax.ppermute(hidden, "yl", SWAP)
    columns, act_copies = lax.optimization_barrier((columns, act_copies))
    act_all = exchange(act_copies, "x")
    hidden_pair = jnp.stack([hidden, hidden_peer])
    hidden_copies = jnp.broadcast_to(hidden_pair[None], (n_x,) + hidden_pair.shape)
    act_all, hidden_copies = lax.optimization_barrier((act_all, hidden_copies))
    act_peer_all = lax.ppermute(act_all, "yl", SWAP)
    hidden_all = exchange(hidden_copies, "x")
    place = jnp.stack([core, lax.axis_index("yl")])
    mine, other = node_sums(place, narrow(columns), hidden_all, act_all, act_peer_all, owned)
    input_grad = input_pass(hidden, weights)
    pairs = mine + lax.ppermute(other, "c", SWAP)
    owned_sums = exchange(pairs, ("yh", "z"))
    grads = jnp.sum(owned_sums, axis=0) / devices_all
    return (input_grad, grads[:owned], grads[owned:])


def solution(mesh):
    fine = Mesh(mesh.devices.reshape(4, 8, 2, 4, 2), AXES)
    by_tokens = P(AXES, None)
    by_rows = P(LOCAL, None)
    owned_rows = P(LOCAL + ("yh", "z", "c"), None)
    return jax.shard_map(
        local,
        mesh=fine,
        in_specs=(by_tokens, by_tokens, by_rows, by_rows, by_rows, by_rows),
        out_specs=(by_tokens, owned_rows, owned_rows),
        check_vma=False,
    )
```

```python
import functools
import math
import jax
import jax.numpy as jnp
from jax import lax
from jax.experimental import pallas as pl
from jax.experimental.pallas import tpu as pltpu
from jax.sharding import Mesh, PartitionSpec as P

QBLOCK = 128
SWAP = ((0, 1), (1, 0))
AXES = ("yh", "z", "c", "x", "yl")
LOCAL = ("x", "yl")
GROUP = ("z", "c")
SHARDS = 2
VMEM_LIMIT = 16 * 1024 * 1024
HIDDEN_LIMIT = 20 * 1024 * 1024


def in_hbm(array):
    return pltpu.with_memory_space_constraint(array, pltpu.HBM)


def exchange(array, axes):
    return lax.all_to_all(array, axes, split_axis=0, concat_axis=0, tiled=True)


def clip_blocks(values):
    parts = []
    for k in range(values.shape[0] // QBLOCK):
        block = values[k * QBLOCK : (k + 1) * QBLOCK]
        mean = jnp.mean(block * block, axis=0, keepdims=True) + 1e-06
        largest = 2.0 * (mean * lax.rsqrt(mean))
        parts.append(jnp.minimum(jnp.maximum(block, -largest), largest))
    return jnp.concatenate(parts, axis=0)


def inner_tanh(v):
    return jnp.tanh(math.sqrt(2.0 / math.pi) * (v + 0.044715 * v * v * v))


def hidden_kernel(
    weights_hbm, tokens_ref, grads_ref, act_hbm, hidden_ref, weights, act, in_sems, out_sems
):
    kinds, n, groups, piece, width = weights.shape
    shard = groups * piece
    arrivals = [
        [
            pltpu.make_async_copy(weights_hbm.at[:, k, kind], weights.at[kind, k], in_sems.at[kind, k])
            for k in range(n)
        ]
        for kind in range(kinds)
    ]
    for copy in arrivals[0] + arrivals[1]:
        copy.start()

    def product(kind, left):
        total = None
        for k in range(n):
            arrivals[kind][k].wait()
            block = weights[kind, k].reshape(shard, width).astype(jnp.bfloat16)
            columns = left[:, k * shard : (k + 1) * shard]
            term = jnp.dot(columns, block, preferred_element_type=jnp.float32)
            total = term if total is None else total + term
        return total

    v = product(0, tokens_ref)
    t = inner_tanh(v)
    act[...] = (0.5 * v * (1.0 + t)).astype(jnp.bfloat16).astype(jnp.float32)
    copies = act_hbm.shape[0]
    departures = [pltpu.make_async_copy(act, act_hbm.at[k], out_sems.at[k]) for k in range(copies)]
    for copy in departures:
        copy.start()
    slope = 0.5 * (1.0 + t) + 0.5 * v * (1.0 - t * t) * math.sqrt(2.0 / math.pi) * (
        1.0 + 3.0 * 0.044715 * v * v
    )
    back = product(1, grads_ref)
    hidden_ref[...] = (back * slope).astype(jnp.bfloat16).astype(jnp.float32)
    for copy in departures:
        copy.wait()


def hidden_pass(weights, tokens, grads, copies):
    groups, n, kinds, piece, width = weights.shape
    rows, depth = tokens.shape
    return pl.pallas_call(
        hidden_kernel,
        in_specs=[
            pl.BlockSpec(memory_space=pltpu.HBM),
            pl.BlockSpec(memory_space=pltpu.VMEM),
            pl.BlockSpec(memory_space=pltpu.VMEM),
        ],
        out_specs=[pl.BlockSpec(memory_space=pltpu.HBM), pl.BlockSpec(memory_space=pltpu.VMEM)],
        out_shape=[
            pltpu.HBM((copies, rows, width), jnp.float32),
            jax.ShapeDtypeStruct((rows, width), jnp.float32),
        ],
        scratch_shapes=[
            pltpu.VMEM((kinds, n, groups, piece, width), jnp.float32),
            pltpu.VMEM((rows, width), jnp.float32),
            pltpu.SemaphoreType.DMA((kinds, n)),
            pltpu.SemaphoreType.DMA((copies,)),
        ],
        compiler_params=pltpu.CompilerParams(vmem_limit_bytes=HIDDEN_LIMIT),
        cost_estimate=pl.CostEstimate(
            flops=4 * rows * depth * width, bytes_accessed=13000000, transcendentals=rows * width
        ),
        name="hidden_pass",
    )(in_hbm(weights), tokens, grads)


def pair_kernel(own_ref, peer_ref, out_hbm, sems):
    copies = [
        pltpu.make_async_copy(source, out_hbm.at[k, j], sems.at[k, j])
        for k in range(out_hbm.shape[0])
        for j, source in enumerate((own_ref, peer_ref))
    ]
    for copy in copies:
        copy.start()
    for copy in copies:
        copy.wait()


def pair_copies(own, peer, copies):
    vmem = pl.BlockSpec(memory_space=pltpu.VMEM)
    return pl.pallas_call(
        pair_kernel,
        in_specs=[vmem, vmem],
        out_specs=pl.BlockSpec(memory_space=pltpu.HBM),
        out_shape=pltpu.HBM((copies, 2) + own.shape, own.dtype),
        scratch_shapes=[pltpu.SemaphoreType.DMA((copies, 2))],
        compiler_params=pltpu.CompilerParams(vmem_limit_bytes=VMEM_LIMIT),
        cost_estimate=pl.CostEstimate(flops=0, bytes_accessed=2000000, transcendentals=0),
        name="pair_copies",
    )(own, peer)


def input_kernel(hidden_ref, weights_ref, out_ref):
    _, shards, _, width = weights_ref.shape
    shard = out_ref.shape[1] // shards
    hidden = hidden_ref[...].astype(jnp.bfloat16)
    for q in range(shards):
        up = weights_ref[:, q].reshape(shard, width).astype(jnp.bfloat16)
        out_ref[:, q * shard : (q + 1) * shard] = lax.dot_general(
            hidden, up, (((1,), (1,)), ((), ())), preferred_element_type=jnp.float32
        ).astype(out_ref.dtype)


def input_pass(hidden, weights):
    groups, n, _, piece, width = weights.shape
    rows = hidden.shape[0]
    depth = groups * n * piece
    return pl.pallas_call(
        input_kernel,
        grid=(n // SHARDS,),
        in_specs=[
            pl.BlockSpec((rows, width), lambda k: (0, 0)),
            pl.BlockSpec((groups, SHARDS, None, piece, width), lambda k: (0, k, 0, 0, 0)),
        ],
        out_specs=pl.BlockSpec((rows, SHARDS * depth // n), lambda k: (0, k)),
        out_shape=jax.ShapeDtypeStruct((rows, depth), jnp.bfloat16),
        compiler_params=pltpu.CompilerParams(vmem_limit_bytes=VMEM_LIMIT),
        cost_estimate=pl.CostEstimate(
            flops=2 * rows * depth * width, bytes_accessed=6000000, transcendentals=0
        ),
        name="input_pass",
    )(hidden, weights)


def piece_kernel(place_ref, up_ref, up_scales_ref, down_ref, down_scales_ref, out_ref):
    piece, width = up_ref.shape
    shard = up_scales_ref.shape[1]
    shape = (piece, shard)
    wanted = lax.broadcasted_iota(jnp.int32, shape, 0) + place_ref[0] * piece
    chosen = wanted == lax.broadcasted_iota(jnp.int32, shape, 1)
    for kind, (codes, scales) in enumerate(((up_ref, up_scales_ref), (down_ref, down_scales_ref))):
        for k in range(width // QBLOCK):
            own = jnp.sum(jnp.where(chosen, scales[k : k + 1], 0.0), axis=1, keepdims=True)
            columns = slice(k * QBLOCK, (k + 1) * QBLOCK)
            product = codes[:, columns].astype(jnp.float32) * own
            for p in range(out_ref.shape[0]):
                out_ref[p, kind, :, columns] = product


def make_pieces(place, n_group, n_local, up_codes, up_scales, down_codes, down_scales):
    shard, width = up_codes.shape
    piece = shard // n_group
    codes = pl.BlockSpec((piece, width), lambda k, place_ref: (place_ref[0], 0))
    scales = pl.BlockSpec(up_scales.T.shape, lambda k, place_ref: (0, 0))
    out = (n_local, 2, piece, width)
    return pl.pallas_call(
        piece_kernel,
        grid_spec=pltpu.PrefetchScalarGridSpec(
            num_scalar_prefetch=1,
            grid=(1,),
            in_specs=[codes, scales, codes, scales],
            out_specs=pl.BlockSpec(out, lambda k, place_ref: (0, 0, 0, 0)),
        ),
        out_shape=jax.ShapeDtypeStruct(out, jnp.float32),
        compiler_params=pltpu.CompilerParams(vmem_limit_bytes=VMEM_LIMIT),
        name="make_pieces",
    )(
        place[None],
        in_hbm(up_codes),
        in_hbm(up_scales.T),
        in_hbm(down_codes),
        in_hbm(down_scales.T),
    )


def narrow_kernel(columns_ref, out_ref):
    out_ref[...] = columns_ref[...].astype(out_ref.dtype)


def narrow(columns):
    n = columns.shape[0]
    block = pl.BlockSpec((n // 2,) + columns.shape[1:], lambda k: (k, 0, 0))
    return pl.pallas_call(
        narrow_kernel,
        grid=(2,),
        in_specs=[block],
        out_specs=block,
        out_shape=jax.ShapeDtypeStruct(columns.shape, jnp.bfloat16),
        compiler_params=pltpu.CompilerParams(vmem_limit_bytes=VMEM_LIMIT),
        cost_estimate=pl.CostEstimate(flops=0, bytes_accessed=12000000, transcendentals=0),
        name="narrow",
    )(columns)


def cut_kernel(tokens_ref, grads_ref, out_ref):
    rows = tokens_ref.shape[0]
    out_ref[:rows] = tokens_ref[...].astype(jnp.float32)
    out_ref[rows:] = grads_ref[...].astype(jnp.float32)


def cut_columns(tokens, grads, n):
    rows, depth = tokens.shape
    cut = pl.BlockSpec((rows, depth // n), lambda k: (0, k))
    return pl.pallas_call(
        cut_kernel,
        grid=(n,),
        in_specs=[cut, cut],
        out_specs=pl.BlockSpec((None, 2 * rows, depth // n), lambda k: (k, 0, 0)),
        out_shape=jax.ShapeDtypeStruct((n, 2 * rows, depth // n), jnp.float32),
        compiler_params=pltpu.CompilerParams(vmem_limit_bytes=VMEM_LIMIT),
        cost_estimate=pl.CostEstimate(flops=0, bytes_accessed=8000000, transcendentals=0),
        name="cut_columns",
    )(tokens, grads)


def node_kernel(place_ref, left, hidden_ref, act_ref, act_peer_ref, mine_ref, other_ref):
    rows, width = act_ref.shape[1:]
    n = left.shape[0]
    totals = [None, None]
    for p in range(n):
        owner = 2 * (p // 2) + lax.rem(place_ref[1] + p, 2)
        rights = (hidden_ref[p // 2, p % 2], (act_peer_ref if p % 2 else act_ref)[p // 2])
        for kind in range(2):
            term = lax.dot_general(
                rights[kind].astype(jnp.bfloat16),
                left[owner, kind * rows : (kind + 1) * rows],
                (((0,), (0,)), ((), ())),
                preferred_element_type=jnp.float32,
            )
            clipped = clip_blocks(term)
            totals[kind] = clipped if totals[kind] is None else totals[kind] + clipped
    owned = mine_ref.shape[1] // 2
    for kind in range(2):
        summed = clip_blocks(totals[kind]).T.reshape(mine_ref.shape[0], 2, owned, width)
        first = place_ref[0] == 0
        part = slice(kind * owned, (kind + 1) * owned)
        mine_ref[:, part] = jnp.where(first, summed[:, 0], summed[:, 1])
        other_ref[:, part] = jnp.where(first, summed[:, 1], summed[:, 0])


def node_sums(place, left, hidden, act, act_peer, owned):
    height = left.shape[2]
    n, rows, width = 2 * act.shape[0], act.shape[1], act.shape[2]
    half = (height // (2 * owned), 2 * owned, width)
    vmem = pl.BlockSpec(memory_space=pltpu.VMEM)
    return pl.pallas_call(
        node_kernel,
        in_specs=[
            pl.BlockSpec(memory_space=pltpu.SMEM),
            vmem,
            vmem,
            vmem,
            vmem,
        ],
        out_specs=[vmem, vmem],
        out_shape=[jax.ShapeDtypeStruct(half, jnp.float32)] * 2,
        compiler_params=pltpu.CompilerParams(vmem_limit_bytes=VMEM_LIMIT),
        cost_estimate=pl.CostEstimate(
            flops=4 * n * rows * height * width, bytes_accessed=9000000, transcendentals=0
        ),
        name="node_sums",
    )(place, left, hidden, act, act_peer)


def local(tokens, out_grad, up_codes, up_scales, down_codes, down_scales):
    n_local = lax.axis_size(LOCAL)
    n_group = lax.axis_size(GROUP)
    devices_all = lax.axis_size(AXES)
    depth = tokens.shape[1]
    owned = depth // devices_all
    core = lax.axis_index("c")

    place = lax.axis_index(GROUP)
    pieces = exchange(
        make_pieces(place, n_group, n_local, up_codes, up_scales, down_codes, down_scales), LOCAL
    )
    pieces, cut = lax.optimization_barrier((pieces, cut_columns(tokens, out_grad, n_local)))
    weights = lax.all_gather(pieces, GROUP, axis=0)
    columns = exchange(cut, LOCAL)
    n_x = lax.axis_size("x")
    act_copies, hidden = hidden_pass(weights, tokens, out_grad, n_x)
    hidden_peer = lax.ppermute(hidden, "yl", SWAP)
    columns, act_copies = lax.optimization_barrier((columns, act_copies))
    act_all = exchange(act_copies, "x")
    hidden_copies = pair_copies(hidden, hidden_peer, n_x)
    act_all, hidden_copies = lax.optimization_barrier((act_all, hidden_copies))
    act_peer_all = lax.ppermute(act_all, "yl", SWAP)
    hidden_all = exchange(hidden_copies, "x")
    place = jnp.stack([core, lax.axis_index("yl")])
    mine, other = node_sums(place, narrow(columns), hidden_all, act_all, act_peer_all, owned)
    input_grad = input_pass(hidden, weights)
    pairs = mine + lax.ppermute(other, "c", SWAP)
    owned_sums = exchange(pairs, ("yh", "z"))
    grads = jnp.sum(owned_sums, axis=0) / devices_all
    return (input_grad, grads[:owned], grads[owned:])


def solution(mesh):
    fine = Mesh(mesh.devices.reshape(4, 8, 2, 4, 2), AXES)
    by_tokens = P(AXES, None)
    by_rows = P(LOCAL, None)
    owned_rows = P(LOCAL + ("yh", "z", "c"), None)
    return jax.shard_map(
        local,
        mesh=fine,
        in_specs=(by_tokens, by_tokens, by_rows, by_rows, by_rows, by_rows),
        out_specs=(by_tokens, owned_rows, owned_rows),
        check_vma=False,
    )
```

```python
import functools
import math
import jax
import jax.numpy as jnp
from jax import lax
from jax.experimental import pallas as pl
from jax.experimental.pallas import tpu as pltpu
from jax.sharding import Mesh, PartitionSpec as P

QBLOCK = 128
SWAP = ((0, 1), (1, 0))
AXES = ("yh", "z", "c", "x", "yl")
LOCAL = ("x", "yl")
GROUP = ("z", "c")
SHARDS = 2
VMEM_LIMIT = 16 * 1024 * 1024
HIDDEN_LIMIT = 20 * 1024 * 1024


def in_hbm(array):
    return pltpu.with_memory_space_constraint(array, pltpu.HBM)


def exchange(array, axes):
    return lax.all_to_all(array, axes, split_axis=0, concat_axis=0, tiled=True)


def clip_blocks(values):
    parts = []
    for k in range(values.shape[0] // QBLOCK):
        block = values[k * QBLOCK : (k + 1) * QBLOCK]
        mean = jnp.mean(block * block, axis=0, keepdims=True) + 1e-06
        largest = 2.0 * (mean * lax.rsqrt(mean))
        parts.append(jnp.minimum(jnp.maximum(block, -largest), largest))
    return jnp.concatenate(parts, axis=0)


def inner_tanh(v):
    return jnp.tanh(math.sqrt(2.0 / math.pi) * (v + 0.044715 * v * v * v))


def hidden_kernel(
    weights_hbm, tokens_ref, grads_ref, act_hbm, hidden_ref, weights, act, in_sems, out_sems
):
    kinds, n, groups, piece, width = weights.shape
    shard = groups * piece
    arrivals = [
        [
            pltpu.make_async_copy(weights_hbm.at[:, k, kind], weights.at[kind, k], in_sems.at[kind, k])
            for k in range(n)
        ]
        for kind in range(kinds)
    ]
    for copy in arrivals[0] + arrivals[1]:
        copy.start()

    def product(kind, left):
        total = None
        for k in range(n):
            arrivals[kind][k].wait()
            block = weights[kind, k].reshape(shard, width).astype(jnp.bfloat16)
            columns = left[:, k * shard : (k + 1) * shard]
            term = jnp.dot(columns, block, preferred_element_type=jnp.float32)
            total = term if total is None else total + term
        return total

    v = product(0, tokens_ref)
    t = inner_tanh(v)
    act[...] = (0.5 * v * (1.0 + t)).astype(jnp.bfloat16).astype(jnp.float32)
    copies = act_hbm.shape[0]
    departures = [pltpu.make_async_copy(act, act_hbm.at[k], out_sems.at[k]) for k in range(copies)]
    for copy in departures:
        copy.start()
    slope = 0.5 * (1.0 + t) + 0.5 * v * (1.0 - t * t) * math.sqrt(2.0 / math.pi) * (
        1.0 + 3.0 * 0.044715 * v * v
    )
    back = product(1, grads_ref)
    hidden_ref[...] = (back * slope).astype(jnp.bfloat16).astype(jnp.float32)
    for copy in departures:
        copy.wait()


def hidden_pass(weights, tokens, grads, copies):
    groups, n, kinds, piece, width = weights.shape
    rows, depth = tokens.shape
    return pl.pallas_call(
        hidden_kernel,
        in_specs=[
            pl.BlockSpec(memory_space=pltpu.HBM),
            pl.BlockSpec(memory_space=pltpu.VMEM),
            pl.BlockSpec(memory_space=pltpu.VMEM),
        ],
        out_specs=[pl.BlockSpec(memory_space=pltpu.HBM), pl.BlockSpec(memory_space=pltpu.VMEM)],
        out_shape=[
            pltpu.HBM((copies, rows, width), jnp.float32),
            jax.ShapeDtypeStruct((rows, width), jnp.float32),
        ],
        scratch_shapes=[
            pltpu.VMEM((kinds, n, groups, piece, width), jnp.float32),
            pltpu.VMEM((rows, width), jnp.float32),
            pltpu.SemaphoreType.DMA((kinds, n)),
            pltpu.SemaphoreType.DMA((copies,)),
        ],
        compiler_params=pltpu.CompilerParams(vmem_limit_bytes=HIDDEN_LIMIT),
        cost_estimate=pl.CostEstimate(
            flops=4 * rows * depth * width, bytes_accessed=13000000, transcendentals=rows * width
        ),
        name="hidden_pass",
    )(in_hbm(weights), tokens, grads)


def pair_kernel(own_ref, peer_ref, out_hbm, sems):
    copies = [
        pltpu.make_async_copy(source, out_hbm.at[k, j], sems.at[k, j])
        for k in range(out_hbm.shape[0])
        for j, source in enumerate((own_ref, peer_ref))
    ]
    for copy in copies:
        copy.start()
    for copy in copies:
        copy.wait()


def pair_copies(own, peer, copies):
    vmem = pl.BlockSpec(memory_space=pltpu.VMEM)
    return pl.pallas_call(
        pair_kernel,
        in_specs=[vmem, vmem],
        out_specs=pl.BlockSpec(memory_space=pltpu.HBM),
        out_shape=pltpu.HBM((copies, 2) + own.shape, own.dtype),
        scratch_shapes=[pltpu.SemaphoreType.DMA((copies, 2))],
        compiler_params=pltpu.CompilerParams(vmem_limit_bytes=VMEM_LIMIT),
        cost_estimate=pl.CostEstimate(flops=0, bytes_accessed=2000000, transcendentals=0),
        name="pair_copies",
    )(own, peer)


def input_kernel(hidden_ref, weights_ref, out_ref):
    _, shards, _, width = weights_ref.shape
    shard = out_ref.shape[1] // shards
    hidden = hidden_ref[...].astype(jnp.bfloat16)
    for q in range(shards):
        up = weights_ref[:, q].reshape(shard, width).astype(jnp.bfloat16)
        out_ref[:, q * shard : (q + 1) * shard] = lax.dot_general(
            hidden, up, (((1,), (1,)), ((), ())), preferred_element_type=jnp.float32
        ).astype(out_ref.dtype)


def input_pass(hidden, weights):
    groups, n, _, piece, width = weights.shape
    rows = hidden.shape[0]
    depth = groups * n * piece
    return pl.pallas_call(
        input_kernel,
        grid=(n // SHARDS,),
        in_specs=[
            pl.BlockSpec((rows, width), lambda k: (0, 0)),
            pl.BlockSpec((groups, SHARDS, None, piece, width), lambda k: (0, k, 0, 0, 0)),
        ],
        out_specs=pl.BlockSpec((rows, SHARDS * depth // n), lambda k: (0, k)),
        out_shape=jax.ShapeDtypeStruct((rows, depth), jnp.bfloat16),
        compiler_params=pltpu.CompilerParams(vmem_limit_bytes=VMEM_LIMIT),
        cost_estimate=pl.CostEstimate(
            flops=2 * rows * depth * width, bytes_accessed=6000000, transcendentals=0
        ),
        name="input_pass",
    )(hidden, weights)


def piece_kernel(place_ref, up_ref, up_scales_ref, down_ref, down_scales_ref, out_ref):
    piece, width = up_ref.shape
    shard = up_scales_ref.shape[1]
    shape = (piece, shard)
    wanted = lax.broadcasted_iota(jnp.int32, shape, 0) + place_ref[0] * piece
    chosen = wanted == lax.broadcasted_iota(jnp.int32, shape, 1)
    for kind, (codes, scales) in enumerate(((up_ref, up_scales_ref), (down_ref, down_scales_ref))):
        for k in range(width // QBLOCK):
            own = jnp.sum(jnp.where(chosen, scales[k : k + 1], 0.0), axis=1, keepdims=True)
            columns = slice(k * QBLOCK, (k + 1) * QBLOCK)
            product = codes[:, columns].astype(jnp.float32) * own
            for p in range(out_ref.shape[0]):
                out_ref[p, kind, :, columns] = product


def make_pieces(place, n_group, n_local, up_codes, up_scales, down_codes, down_scales):
    shard, width = up_codes.shape
    piece = shard // n_group
    codes = pl.BlockSpec((piece, width), lambda k, place_ref: (place_ref[0], 0))
    scales = pl.BlockSpec(up_scales.T.shape, lambda k, place_ref: (0, 0))
    out = (n_local, 2, piece, width)
    return pl.pallas_call(
        piece_kernel,
        grid_spec=pltpu.PrefetchScalarGridSpec(
            num_scalar_prefetch=1,
            grid=(1,),
            in_specs=[codes, scales, codes, scales],
            out_specs=pl.BlockSpec(out, lambda k, place_ref: (0, 0, 0, 0)),
        ),
        out_shape=jax.ShapeDtypeStruct(out, jnp.float32),
        compiler_params=pltpu.CompilerParams(vmem_limit_bytes=VMEM_LIMIT),
        name="make_pieces",
    )(
        place[None],
        in_hbm(up_codes),
        in_hbm(up_scales.T),
        in_hbm(down_codes),
        in_hbm(down_scales.T),
    )


def narrow_kernel(columns_ref, out_ref):
    out_ref[...] = columns_ref[...].astype(out_ref.dtype)


def narrow(columns):
    n = columns.shape[0]
    block = pl.BlockSpec((n // 2,) + columns.shape[1:], lambda k: (k, 0, 0))
    return pl.pallas_call(
        narrow_kernel,
        grid=(2,),
        in_specs=[block],
        out_specs=block,
        out_shape=jax.ShapeDtypeStruct(columns.shape, jnp.bfloat16),
        compiler_params=pltpu.CompilerParams(vmem_limit_bytes=VMEM_LIMIT),
        cost_estimate=pl.CostEstimate(flops=0, bytes_accessed=12000000, transcendentals=0),
        name="narrow",
    )(columns)


def cut_kernel(tokens_ref, grads_ref, out_ref):
    rows = tokens_ref.shape[0]
    out_ref[:rows] = tokens_ref[...].astype(jnp.float32)
    out_ref[rows:] = grads_ref[...].astype(jnp.float32)


def cut_columns(tokens, grads, n):
    rows, depth = tokens.shape
    cut = pl.BlockSpec((rows, depth // n), lambda k: (0, k))
    return pl.pallas_call(
        cut_kernel,
        grid=(n,),
        in_specs=[cut, cut],
        out_specs=pl.BlockSpec((None, 2 * rows, depth // n), lambda k: (k, 0, 0)),
        out_shape=jax.ShapeDtypeStruct((n, 2 * rows, depth // n), jnp.float32),
        compiler_params=pltpu.CompilerParams(vmem_limit_bytes=VMEM_LIMIT),
        cost_estimate=pl.CostEstimate(flops=0, bytes_accessed=8000000, transcendentals=0),
        name="cut_columns",
    )(tokens, grads)


def node_kernel(
    place_ref, left, hidden_hbm, act_ref, act_peer_hbm, mine_ref, other_ref, hidden, act_peer, sems
):
    n_x, rows, width = act_ref.shape
    copies = [
        [pltpu.make_async_copy(act_peer_hbm.at[k], act_peer.at[k], sems.at[0, k]) for k in range(n_x)],
        [pltpu.make_async_copy(hidden_hbm.at[k], hidden.at[k], sems.at[1, k]) for k in range(n_x)],
    ]
    for copy in copies[0] + copies[1]:
        copy.start()

    def term(owner, kind, right):
        return clip_blocks(
            lax.dot_general(
                right.astype(jnp.bfloat16),
                left[owner, kind * rows : (kind + 1) * rows],
                (((0,), (0,)), ((), ())),
                preferred_element_type=jnp.float32,
            )
        )

    def finish(kind, total):
        owned = mine_ref.shape[1] // 2
        summed = clip_blocks(total).T.reshape(mine_ref.shape[0], 2, owned, width)
        first = place_ref[0] == 0
        part = slice(kind * owned, (kind + 1) * owned)
        mine_ref[:, part] = jnp.where(first, summed[:, 0], summed[:, 1])
        other_ref[:, part] = jnp.where(first, summed[:, 1], summed[:, 0])

    own = place_ref[1]
    peer = 1 - own
    total = term(own, 1, act_ref[0])
    for k in range(1, n_x):
        total += term(2 * k + own, 1, act_ref[k])
    for k in range(n_x):
        copies[0][k].wait()
        total += term(2 * k + peer, 1, act_peer[k])
    finish(1, total)
    total = None
    for k in range(n_x):
        copies[1][k].wait()
        pair = term(2 * k + own, 0, hidden[k, 0]) + term(2 * k + peer, 0, hidden[k, 1])
        total = pair if total is None else total + pair
    finish(0, total)


def node_sums(place, left, hidden, act, act_peer, owned):
    height = left.shape[2]
    n, rows, width = 2 * act.shape[0], act.shape[1], act.shape[2]
    half = (height // (2 * owned), 2 * owned, width)
    vmem = pl.BlockSpec(memory_space=pltpu.VMEM)
    return pl.pallas_call(
        node_kernel,
        in_specs=[
            pl.BlockSpec(memory_space=pltpu.SMEM),
            vmem,
            pl.BlockSpec(memory_space=pltpu.HBM),
            vmem,
            pl.BlockSpec(memory_space=pltpu.HBM),
        ],
        out_specs=[vmem, vmem],
        out_shape=[jax.ShapeDtypeStruct(half, jnp.float32)] * 2,
        scratch_shapes=[
            pltpu.VMEM(hidden.shape, hidden.dtype),
            pltpu.VMEM(act_peer.shape, act_peer.dtype),
            pltpu.SemaphoreType.DMA((2, act.shape[0])),
        ],
        compiler_params=pltpu.CompilerParams(vmem_limit_bytes=VMEM_LIMIT),
        cost_estimate=pl.CostEstimate(
            flops=4 * n * rows * height * width, bytes_accessed=9000000, transcendentals=0
        ),
        name="node_sums",
    )(place, left, in_hbm(hidden), act, in_hbm(act_peer))


def local(tokens, out_grad, up_codes, up_scales, down_codes, down_scales):
    n_local = lax.axis_size(LOCAL)
    n_group = lax.axis_size(GROUP)
    devices_all = lax.axis_size(AXES)
    depth = tokens.shape[1]
    owned = depth // devices_all
    core = lax.axis_index("c")

    place = lax.axis_index(GROUP)
    pieces = exchange(
        make_pieces(place, n_group, n_local, up_codes, up_scales, down_codes, down_scales), LOCAL
    )
    pieces, cut = lax.optimization_barrier((pieces, cut_columns(tokens, out_grad, n_local)))
    weights = lax.all_gather(pieces, GROUP, axis=0)
    columns = exchange(cut, LOCAL)
    n_x = lax.axis_size("x")
    act_copies, hidden = hidden_pass(weights, tokens, out_grad, n_x)
    hidden_peer = lax.ppermute(hidden, "yl", SWAP)
    columns, act_copies = lax.optimization_barrier((columns, act_copies))
    act_all = exchange(act_copies, "x")
    hidden_copies = pair_copies(hidden, hidden_peer, n_x)
    act_all, hidden_copies = lax.optimization_barrier((act_all, hidden_copies))
    act_peer_all = lax.ppermute(act_all, "yl", SWAP)
    hidden_all = exchange(hidden_copies, "x")
    place = jnp.stack([core, lax.axis_index("yl")])
    mine, other = node_sums(place, narrow(columns), hidden_all, act_all, act_peer_all, owned)
    input_grad = input_pass(hidden, weights)
    pairs = mine + lax.ppermute(other, "c", SWAP)
    owned_sums = exchange(pairs, ("yh", "z"))
    grads = jnp.sum(owned_sums, axis=0) / devices_all
    return (input_grad, grads[:owned], grads[owned:])


def solution(mesh):
    fine = Mesh(mesh.devices.reshape(4, 8, 2, 4, 2), AXES)
    by_tokens = P(AXES, None)
    by_rows = P(LOCAL, None)
    owned_rows = P(LOCAL + ("yh", "z", "c"), None)
    return jax.shard_map(
        local,
        mesh=fine,
        in_specs=(by_tokens, by_tokens, by_rows, by_rows, by_rows, by_rows),
        out_specs=(by_tokens, owned_rows, owned_rows),
        check_vma=False,
    )
```
